128 devices in a mesh: sn: 32 (over x, y, core), blk: 4 (over z).
Axes of the slice: x: 4, y: 4, z: 4, core: 2. Of those that a mesh axis runs over, the one named last changes fastest.
Arguments:
- root_inverse: float32 [8192, 8192], P('sn'), as said below
- structure: int32 [32, 4], replicated, may hold values from 0 to 31, as said below
- panel_one: float32 [32, 1024, 256], P('sn', 'blk'), may hold values from -0.375 to 0.375
- inverse_one: float32 [32, 256, 256], P('sn'), as said below
- parent_two: float32 [32, 256, 256], P('sn'), may hold values from -0.375 to 0.375
- panel_two: float32 [32, 1024, 256], P('sn', 'blk'), may hold values from -0.375 to 0.375
- inverse_two: float32 [32, 256, 256], P('sn'), as said below
Outputs:
- sigma_diag_one: float32 [32, 256, 256], P('sn')
- sigma_off_one: float32 [32, 1024, 256], P('sn', 'blk')
- sigma_diag_two: float32 [32, 256, 256], P('sn')
- sigma_par_two: float32 [32, 256, 256], P('sn')
- sigma_root_two: float32 [32, 1024, 256], P('sn', 'blk')
The draws below stay inside these ranges and needn't reach their ends.
Inputs may be any that keep to these rules, and one draw needn't show every extreme that they name: `structure`: each row holds 4 distinct block indices. `inverse_one`: lower triangular; diagonal between 0.5 and 1.5. `inverse_two`: lower triangular; diagonal between 0.5 and 1.5. `root_inverse`: Symmetric.
All inputs are finite; a program needn't handle non-finite values.
Results may differ from the reference program's by a relative error of at most 0.00011.
Values sent between devices are 32-bit elements; how exact they have to be, the bound alone decides.
A program may use at most 128 MiB of HBM per device.

```python
import math
import jax
import jax.numpy as jnp
from jax import lax

B = 256
K = 4
RB = 32
SUPER = 32


def draw_root_inverse(key, part):
    total = RB * B
    first, second, third = jax.random.split(key, 3)
    base = jax.random.normal(first, (total, total), jnp.float32)
    scale = jnp.exp(jax.random.uniform(second, (total,), jnp.float32, 0.0, math.log(3.0)))
    coupling = (base + base.T) * (1.4142 / math.sqrt(total))
    diagonal = jax.random.uniform(third, (total,), jnp.float32, 1.0, 4.0)
    rows = jnp.arange(total)[:, None]
    cols = jnp.arange(total)[None, :]
    middle = jnp.where(rows == cols, diagonal[:, None], coupling)
    return scale[:, None] * middle * scale[None, :]


def draw_structure(key, part):
    first, second = jax.random.split(key, 2)
    order = jax.random.permutation(first, RB)
    starts = jax.random.randint(second, (SUPER,), 0, RB)
    rows = jnp.arange(SUPER)
    starts = jnp.where(rows < RB // K, rows * K, starts)
    places = (starts[:, None] + jnp.arange(K)[None, :]) % RB
    return order[places].astype(jnp.int32)


def lower_inverse(key):
    first, second = jax.random.split(key, 2)
    body_part = jax.random.normal(first, (SUPER, B, B), jnp.float32) * (0.5 / math.sqrt(B))
    diagonal = jax.random.uniform(second, (SUPER, B), jnp.float32, 0.5, 1.5)
    rows = jnp.arange(B)[:, None]
    cols = jnp.arange(B)[None, :]
    strict = jnp.where(rows > cols, body_part, 0.0)
    return jnp.where(rows == cols, diagonal[:, :, None], strict)


def draw_inverse_one(key, part):
    return lower_inverse(jax.random.fold_in(key, 11))


def draw_inverse_two(key, part):
    return lower_inverse(jax.random.fold_in(key, 23))


def steps_of(rng, dims, cuts, smallest, largest):
    gain, own = 1.0, jax.random.fold_in(rng, 6)
    for position, parts in cuts:
        draws = jnp.exp(jax.random.uniform(jax.random.fold_in(own, position), (parts,), jnp.float32, smallest / len(cuts), largest / len(cuts)))
        gain = gain * jnp.repeat(draws, dims[position] // parts).reshape([-1 if axis == position else 1 for axis in range(len(dims))])
    return gain


def bell_draw(own_key, dims, scale, limit, pieces=(), held_as=jnp.bfloat16):
    gain = steps_of(own_key, dims, pieces, -0.22, 0.18) if pieces else 1.0
    entries = jax.random.normal(own_key, dims, jnp.float32) * scale * gain
    return jnp.minimum(jnp.maximum(entries, -limit), limit).astype(held_as)


def setup_inputs(seed: int = 0) -> dict:
    streams_of = jax.random.split(jax.random.key(seed), 8)
    root_inverse = draw_root_inverse(jax.random.fold_in(streams_of[7], 71), 0)
    structure = draw_structure(jax.random.fold_in(streams_of[7], 71), 0)
    panel_one = bell_draw(streams_of[2], (SUPER, K * B, B), B ** -0.5, 0.375, ((0, 32), (1, 4)), jnp.float32)
    inverse_one = draw_inverse_one(jax.random.fold_in(streams_of[7], 71), 0)
    parent_two = bell_draw(streams_of[4], (SUPER, B, B), B ** -0.5, 0.375, ((0, 32),), jnp.float32)
    panel_two = bell_draw(streams_of[5], (SUPER, K * B, B), B ** -0.5, 0.375, ((0, 32), (1, 4)), jnp.float32)
    inverse_two = draw_inverse_two(jax.random.fold_in(streams_of[7], 71), 0)
    return dict(root_inverse=root_inverse, structure=structure, panel_one=panel_one, inverse_one=inverse_one, parent_two=parent_two, panel_two=panel_two, inverse_two=inverse_two)


def product(left, right):
    return jnp.dot(left, right, precision=lax.Precision.HIGHEST, preferred_element_type=jnp.float32)


def reference(root_inverse, structure, panel_one, inverse_one, parent_two, panel_two, inverse_two):
    blocks = root_inverse.reshape(RB, B, RB, B)

    def single(items):
        listed, lower_one, inv_one, upper_two, lower_two, inv_two = items
        picked = jnp.take(blocks, listed, axis=0)
        picked = jnp.take(picked, listed, axis=2).reshape(K * B, K * B)
        u_one = product(lower_one, inv_one)
        u_root = product(lower_two, inv_two)
        u_par = product(upper_two, inv_two)
        w_all = product(picked, jnp.concatenate([u_one, u_root], axis=1))
        w_one = w_all[:, :B]
        w_two = w_all[:, B:]
        off_one = -w_one
        diag_one = product(inv_one.T, inv_one) + product(u_one.T, w_one)
        root_two = -(w_two + product(off_one, u_par))
        par_two = -(product(off_one.T, u_root) + product(diag_one, u_par))
        diag_two = product(inv_two.T, inv_two) - product(u_par.T, par_two) - product(u_root.T, root_two)
        return diag_one, off_one, diag_two, par_two, root_two

    outs = lax.map(single, (structure, panel_one, inverse_one, parent_two, panel_two, inverse_two))
    return (outs[0], outs[1], outs[2], outs[3], outs[4])
```

```python
import functools

import jax
import jax.numpy as jnp
from jax import lax
from jax.experimental import pallas as pl
from jax.experimental.pallas import tpu as pltpu
from jax.sharding import PartitionSpec as P

MESH = pl.DeviceIdType.MESH
SIDE = 4
CORES = 2
POSITIONS = 4
PAIRS = tuple((i, k) for i in range(POSITIONS) for k in range(i, POSITIONS))
NP = len(PAIRS)
BLOCKS = 32
NEAR = BLOCKS // 2 + 1


def locate(a, b):
    d = jnp.bitwise_and(b - a + BLOCKS, BLOCKS - 1)
    swap = d >= NEAR
    return jnp.where(swap, b, a), jnp.where(swap, BLOCKS - d, d), swap


def place(row):
    return row // (SIDE * CORES), lax.rem(row // CORES, SIDE), lax.rem(row, CORES)


def exchange_kernel(
    pairs_ref, root, panel_one, panel_two, zed, panels,
    ag_a, ag_b, send_a, send_b, recv_a, recv_b,
    own_sem, pan_local, pan_send, pan_recv, ring_send, ring_recv,
    core_send, core_recv, sel_send, sel_recv, z_send, z_recv,
):
    width = panel_one.shape[0]
    quarter = width // SIDE
    half = quarter // 2
    sn = lax.axis_index("sn")
    z = lax.axis_index("blk")
    x, y, c = place(sn)

    def at(xx, yy, cc):
        return (xx * SIDE + yy) * CORES + cc

    def turn(v, o):
        return lax.rem(v + o, SIDE)

    x_dev = [(at(turn(x, o), y, c), z) for o in range(SIDE)]
    y_dev = [(at(x, turn(y, o), c), z) for o in range(SIDE)]
    z_dev = [(sn, turn(z, o)) for o in range(SIDE)]
    twin = (at(x, y, 1 - c), z)

    slot_a = x * CORES + c
    slot_b = y * CORES + c
    loads = []
    for h, (buf, slot) in enumerate(((ag_a, slot_a), (ag_b, slot_b))):
        for d in range(NEAR):
            col = lax.rem(sn + d, BLOCKS)
            cp = pltpu.make_async_copy(
                root.at[pl.ds(pl.multiple_of(z * quarter + h * half, half), half), pl.ds(pl.multiple_of(col * width, width), width)],
                buf.at[slot * NEAR + d],
                own_sem.at[h, d],
            )
            cp.start()
            loads.append(cp)
    pan = []
    for n, src in enumerate((panel_one, panel_two)):
        cp = pltpu.make_async_copy(src, panels.at[z, n], pan_local.at[n])
        cp.start()
        pan.append(cp)

    barrier = pltpu.get_barrier_semaphore()
    partners = x_dev[1:] + y_dev[1:] + z_dev[1:] + [twin]
    for dev in partners:
        pl.semaphore_signal(barrier, inc=1, device_id=dev, device_id_type=MESH)
    pl.semaphore_wait(barrier, len(partners))

    def remote(src, dst, ssem, rsem, dev):
        return pltpu.make_async_remote_copy(
            src_ref=src, dst_ref=dst, send_sem=ssem, recv_sem=rsem, device_id=dev, device_id_type=MESH
        )

    pan_out = []
    for o in range(1, SIDE):
        for n, src in enumerate((panel_one, panel_two)):
            cp = remote(src, panels.at[z, n], pan_send.at[o - 1, n], pan_recv.at[o - 1, n], z_dev[o])
            cp.start()
            pan_out.append(cp)

    lanes = []
    for h, (buf, pos, devs) in enumerate(((ag_a, x, x_dev), (ag_b, y, y_dev))):
        for cp in loads[h * NEAR:(h + 1) * NEAR]:
            cp.wait()

        def piece(o, lo=0, n=NEAR, buf=buf, pos=pos):
            return buf.at[pl.ds((turn(pos, o) * CORES + c) * NEAR + lo, n)]

        def theirs(o, lo=0, n=NEAR, buf=buf, pos=pos):
            return buf.at[pl.ds((turn(pos, o) * CORES + (1 - c)) * NEAR + lo, n)]

        up = remote(piece(0), piece(0), ring_send.at[h, 0], ring_recv.at[h, 0], devs[1])
        down = remote(piece(0), piece(0), ring_send.at[h, 1], ring_recv.at[h, 1], devs[3])
        side = remote(piece(0), piece(0), core_send.at[h, 0], core_recv.at[h, 0], twin)
        up.start()
        down.start()
        side.start()
        lanes.append((piece, theirs, up, down, side, devs))

    split = (NEAR + 1) // 2
    spans = ((0, split), (split, NEAR - split))
    started = []
    for h, (piece, theirs, up, down, side, devs) in enumerate(lanes):
        remote(piece(3), piece(3), ring_send.at[h, 0], ring_recv.at[h, 0], devs[1]).wait_recv()
        f_up = remote(piece(3, *spans[0]), piece(3, *spans[0]), ring_send.at[h, 2], ring_recv.at[h, 2], devs[1])
        f_up.start()
        s_up = remote(piece(3), piece(3), core_send.at[h, 1], core_recv.at[h, 1], twin)
        s_up.start()
        remote(piece(1), piece(1), ring_send.at[h, 1], ring_recv.at[h, 1], devs[3]).wait_recv()
        f_down = remote(piece(1, *spans[1]), piece(1, *spans[1]), ring_send.at[h, 3], ring_recv.at[h, 3], devs[3])
        f_down.start()
        s_down = remote(piece(1), piece(1), core_send.at[h, 2], core_recv.at[h, 2], twin)
        s_down.start()
        started.append([up, down, side, f_up, s_up, f_down, s_down])
    for h, (piece, theirs, up, down, side, devs) in enumerate(lanes):
        for part in range(2):
            remote(piece(2, *spans[part]), piece(2, *spans[part]), ring_send.at[h, 2 + part], ring_recv.at[h, 2 + part], devs[1]).wait_recv()
            s = remote(piece(2, *spans[part]), piece(2, *spans[part]), core_send.at[h, 3 + part], core_recv.at[h, 3 + part], twin)
            s.start()
            started[h].append(s)

    sel = []
    for h, (buf, send, recv, devs, pos, other) in enumerate(
        ((ag_a, send_a, recv_a, y_dev, y, x), (ag_b, send_b, recv_b, x_dev, x, y))
    ):
        piece, theirs = lanes[h][:2]
        for n, (o, lo, cnt) in enumerate(((0, 0, NEAR), (3, 0, NEAR), (1, 0, NEAR), (2, *spans[0]), (2, *spans[1]))):
            remote(theirs(o, lo, cnt), theirs(o, lo, cnt), core_send.at[h, n], core_recv.at[h, n], twin).wait_recv()
        for o in (2, 1, 3, 0):
            to = turn(pos, o)
            item = at(other, to, c) if h == 0 else at(to, other, c)

            def pick(p, carry, h=h, o=o, item=item, buf=buf, send=send, recv=recv, pos=pos):
                i = jnp.where(p < 4, 0, jnp.where(p < 7, 1, jnp.where(p < 9, 2, 3)))
                k = jnp.where(p < 4, p, jnp.where(p < 7, p - 3, jnp.where(p < 9, p - 5, 3)))
                row, dist, _ = locate(pairs_ref[item, i], pairs_ref[item, k])
                rx, ry, rc = place(row)
                slot = ((rx if h == 0 else ry) * CORES + rc) * NEAR + dist
                got = buf[slot]
                if o == 0:
                    recv[pos * NP + p] = got
                else:
                    send[(o - 1) * NP + p] = got
                return carry

            lax.fori_loop(0, NP, pick, 0)
            if o:
                cp = remote(
                    send.at[pl.ds((o - 1) * NP, NP)], recv.at[pl.ds(pos * NP, NP)],
                    sel_send.at[h, o - 1], sel_recv.at[h, o - 1], devs[o],
                )
                cp.start()
                sel.append(cp)
    for h, (send, recv, devs, pos) in enumerate(((send_a, recv_a, y_dev, y), (send_b, recv_b, x_dev, x))):
        for o in range(1, SIDE):
            frm = turn(pos, SIDE - o)
            remote(
                send.at[pl.ds((o - 1) * NP, NP)], recv.at[pl.ds(frm * NP, NP)],
                sel_send.at[h, o - 1], sel_recv.at[h, o - 1], devs[o],
            ).wait_recv()

    def keep(p, carry):
        i = jnp.where(p < 4, 0, jnp.where(p < 7, 1, jnp.where(p < 9, 2, 3)))
        k = jnp.where(p < 4, p, jnp.where(p < 7, p - 3, jnp.where(p < 9, p - 5, 3)))
        row, _, _ = locate(pairs_ref[sn, i], pairs_ref[sn, k])
        rx, ry, _ = place(row)
        zed[z * NP + p, 0:half] = recv_a[ry * NP + p]
        zed[z * NP + p, half:quarter] = recv_b[rx * NP + p]
        return carry

    lax.fori_loop(0, NP, keep, 0)

    def zpart(o, lo=0, n=NP):
        return zed.at[pl.ds(turn(z, o) * NP + lo, n)]

    zspans = ((0, NP // 2), (NP // 2, NP - NP // 2))
    zup = remote(zpart(0), zpart(0), z_send.at[0], z_recv.at[0], z_dev[1])
    zdown = remote(zpart(0), zpart(0), z_send.at[1], z_recv.at[1], z_dev[3])
    zup.start()
    zdown.start()
    remote(zpart(3), zpart(3), z_send.at[0], z_recv.at[0], z_dev[1]).wait_recv()
    fup = remote(zpart(3, *zspans[0]), zpart(3, *zspans[0]), z_send.at[2], z_recv.at[2], z_dev[1])
    fup.start()
    remote(zpart(1), zpart(1), z_send.at[1], z_recv.at[1], z_dev[3]).wait_recv()
    fdown = remote(zpart(1, *zspans[1]), zpart(1, *zspans[1]), z_send.at[3], z_recv.at[3], z_dev[3])
    fdown.start()
    for part in range(2):
        remote(zpart(2, *zspans[part]), zpart(2, *zspans[part]), z_send.at[2 + part], z_recv.at[2 + part], z_dev[1]).wait_recv()
    for o in range(1, SIDE):
        for n, src in enumerate((panel_one, panel_two)):
            remote(src, panels.at[turn(z, SIDE - o), n], pan_send.at[o - 1, n], pan_recv.at[o - 1, n], z_dev[o]).wait_recv()
    for cp in pan:
        cp.wait()
    for cp in pan_out + started[0] + started[1] + sel + [zup, zdown, fup, fdown]:
        cp.wait_send()


def exchange(structure, root, panel_one, panel_two):
    width = panel_one.shape[0]
    quarter, half = width // SIDE, width // SIDE // 2
    f32 = jnp.float32
    dma = pltpu.SemaphoreType.DMA
    anywhere = pl.BlockSpec(memory_space=pl.ANY)
    return pl.pallas_call(
        exchange_kernel,
        out_shape=(
            jax.ShapeDtypeStruct((SIDE * NP, quarter, width), f32),
            jax.ShapeDtypeStruct((SIDE, 2, width, width), f32),
        ),
        in_specs=[pl.BlockSpec(memory_space=pltpu.SMEM), anywhere, anywhere, anywhere],
        out_specs=(pl.BlockSpec(memory_space=pltpu.VMEM), anywhere),
        scratch_shapes=[
            pltpu.VMEM((SIDE * CORES * NEAR, half, width), f32),
            pltpu.VMEM((SIDE * CORES * NEAR, half, width), f32),
            pltpu.VMEM(((SIDE - 1) * NP, half, width), f32),
            pltpu.VMEM(((SIDE - 1) * NP, half, width), f32),
            pltpu.VMEM((SIDE * NP, half, width), f32),
            pltpu.VMEM((SIDE * NP, half, width), f32),
            dma((2, NEAR)),
            dma((2,)),
            dma((SIDE - 1, 2)),
            dma((SIDE - 1, 2)),
            dma((2, 4)),
            dma((2, 4)),
            dma((2, 5)),
            dma((2, 5)),
            dma((2, SIDE - 1)),
            dma((2, SIDE - 1)),
            dma((4,)),
            dma((4,)),
        ],
        compiler_params=pltpu.CompilerParams(
            collective_id=0, has_side_effects=True, vmem_limit_bytes=40 * 2**20
        ),
        name="exchange",
    )(structure, root, panel_one, panel_two)


def parts(v):
    high = v.astype(jnp.bfloat16)
    return high, (v - high.astype(jnp.float32)).astype(jnp.bfloat16)


def mul(a, b, ca=1, cb=0):
    dims = (((ca,), (cb,)), ((), ()))
    dot = functools.partial(lax.dot_general, dimension_numbers=dims, preferred_element_type=jnp.float32)
    return dot(a[0], b[0]) + (dot(a[0], b[1]) + dot(a[1], b[0]))


def finish_kernel(
    structure, zed, panels, inverse_one, parent, inverse_two,
    diag_one, off_one, diag_two, par_two, root_two,
    u_high, u_low, w,
):
    width = inverse_one.shape[0]
    sn = lax.axis_index("sn")
    z = lax.axis_index("blk")
    inv_one = parts(inverse_one[...])
    inv_two = parts(inverse_two[...])
    for k in range(POSITIONS):
        for n, inv in enumerate((inv_one, inv_two)):
            high, low = parts(mul(parts(panels[k, n]), inv))
            u_high[k, :, n * width:(n + 1) * width] = high
            u_low[k, :, n * width:(n + 1) * width] = low
    u_par = parts(mul(parts(parent[...]), inv_two))
    w[...] = jnp.zeros_like(w)
    for p, (i, k) in enumerate(PAIRS):
        block = jnp.concatenate([zed[q * NP + p] for q in range(SIDE)], axis=0)
        block = parts(block)
        if i == k:
            w[i] += mul(block, (u_high[i], u_low[i]))
            continue
        _, _, swap = locate(structure[sn, i], structure[sn, k])
        major = jnp.where(swap, k, i)
        minor = jnp.where(swap, i, k)
        w[major] += mul(block, (u_high[minor], u_low[minor]))
        w[minor] += mul(block, (u_high[major], u_low[major]), 0, 0)
    uu_one = uu_mixed = uu_two = 0.0
    for k in range(POSITIONS):
        one = (u_high[k, :, :width], u_low[k, :, :width])
        two = (u_high[k, :, width:], u_low[k, :, width:])
        w_one = parts(w[k, :, :width])
        w_two = parts(w[k, :, width:])
        uu_one = uu_one + mul(one, w_one, 0, 0)
        uu_mixed = uu_mixed + mul(two, w_one, 0, 0)
        uu_two = uu_two + mul(two, w_two, 0, 0)
    d_one = mul(inv_one, inv_one, 0, 0) + uu_one
    diag_one[...] = d_one
    own_one = w[z, :, :width]
    off_one[...] = -own_one
    root_two[...] = mul(parts(own_one), u_par) - w[z, :, width:]
    p_two = uu_mixed.T - mul(parts(d_one), u_par)
    par_two[...] = p_two
    child = mul(parts(uu_mixed), u_par) - uu_two
    diag_two[...] = mul(inv_two, inv_two, 0, 0) - mul(u_par, parts(p_two), 0, 0) - child


def finish(structure, zed, panels, inverse_one, parent, inverse_two):
    width = inverse_one.shape[0]
    vmem = pl.BlockSpec(memory_space=pltpu.VMEM)
    square = jax.ShapeDtypeStruct((width, width), jnp.float32)
    return pl.pallas_call(
        finish_kernel,
        out_shape=(square,) * 5,
        in_specs=[pl.BlockSpec(memory_space=pltpu.SMEM)] + [vmem] * 5,
        out_specs=(vmem,) * 5,
        scratch_shapes=[
            pltpu.VMEM((POSITIONS, width, 2 * width), jnp.bfloat16),
            pltpu.VMEM((POSITIONS, width, 2 * width), jnp.bfloat16),
            pltpu.VMEM((POSITIONS, width, 2 * width), jnp.float32),
        ],
        compiler_params=pltpu.CompilerParams(vmem_limit_bytes=40 * 2**20),
        name="finish",
    )(structure, zed, panels, inverse_one, parent, inverse_two)


def per_device(root_inverse, structure, panel_one, inverse_one, parent_two, panel_two, inverse_two):
    zed, panels = exchange(structure, root_inverse, panel_one[0], panel_two[0])
    outs = finish(structure, zed, panels, inverse_one[0], parent_two[0], inverse_two[0])
    return tuple(out[None] for out in outs)


def solution(mesh):
    return jax.shard_map(
        per_device,
        mesh=mesh,
        in_specs=(
            P("sn", None),
            P(),
            P("sn", "blk", None),
            P("sn", None, None),
            P("sn", None, None),
            P("sn", "blk", None),
            P("sn", None, None),
        ),
        out_specs=(
            P("sn", None, None),
            P("sn", "blk", None),
            P("sn", None, None),
            P("sn", None, None),
            P("sn", "blk", None),
        ),
        check_vma=False,
    )
```

```python
import functools

import jax
import jax.numpy as jnp
from jax import lax
from jax.experimental import pallas as pl
from jax.experimental.pallas import tpu as pltpu
from jax.sharding import PartitionSpec as P

MESH = pl.DeviceIdType.MESH
SIDE = 4
CORES = 2
POSITIONS = 4
PAIRS = tuple((i, k) for i in range(POSITIONS) for k in range(i, POSITIONS))
NP = len(PAIRS)
BLOCKS = 32
NEAR = BLOCKS // 2 + 1


def locate(a, b):
    d = jnp.bitwise_and(b - a + BLOCKS, BLOCKS - 1)
    swap = d >= NEAR
    return jnp.where(swap, b, a), jnp.where(swap, BLOCKS - d, d), swap


def parts(v):
    high = v.astype(jnp.bfloat16)
    return high, (v - high.astype(jnp.float32)).astype(jnp.bfloat16)


def mul(a, b, ca=1, cb=0):
    dims = (((ca,), (cb,)), ((), ()))
    dot = functools.partial(lax.dot_general, dimension_numbers=dims, preferred_element_type=jnp.float32)
    return dot(a[0], b[0]) + (dot(a[0], b[1]) + dot(a[1], b[0]))


def place(row):
    return row // (SIDE * CORES), lax.rem(row // CORES, SIDE), lax.rem(row, CORES)


def exchange_kernel(
    structure, root, panel_one, panel_two, inverse_one, parent, inverse_two,
    own_w, diag_one, mixed, rest_two, par,
    zed, loaded, u_all, u_high, u_low, w, table, rows, ag_a, ag_b, main_out, main_in, own_in, relay_out, relay_in,
    root_sem, load_sem, pan_send, pan_recv, pan_fsend, pan_frecv,
    ring_send, ring_recv, fwd_send, fwd_recv, core_send, core_recv,
    relay_send, relay_recv, main_send, main_recv, z_send, z_recv, zf_send, zf_recv,
):
    width = panel_one.shape[0]
    quarter = width // SIDE
    half = quarter // 2
    sn = lax.axis_index("sn")
    z = lax.axis_index("blk")
    x, y, c = place(sn)

    def at(xx, yy, cc):
        return (xx * SIDE + yy) * CORES + cc

    def turn(v, o):
        return lax.rem(v + o, SIDE)

    x_dev = [(at(turn(x, o), y, c), z) for o in range(SIDE)]
    y_dev = [(at(x, turn(y, o), c), z) for o in range(SIDE)]
    z_dev = [(sn, turn(z, o)) for o in range(SIDE)]
    twin = (at(x, y, 1 - c), z)
    UP, DOWN = 0, 1
    BELOW, ABOVE = 3, 1
    step = (1, 3)

    own_rows = pltpu.make_async_copy(
        root.at[pl.ds(pl.multiple_of(z * quarter, quarter), quarter), :], rows, root_sem
    )
    own_rows.start()
    loads = [
        pltpu.make_async_copy(src, loaded.at[n], load_sem.at[n])
        for n, src in enumerate((panel_one, inverse_one, panel_two, inverse_two, parent))
    ]
    for cp in loads:
        cp.start()

    barrier = pltpu.get_barrier_semaphore()
    partners = [x_dev[1], x_dev[3], y_dev[1], y_dev[3], z_dev[1], z_dev[3], twin]
    for dev in partners:
        pl.semaphore_signal(barrier, inc=1, device_id=dev, device_id_type=MESH)
    pl.semaphore_wait(barrier, len(partners))

    sent = []

    def remote(src, dst, ssem, rsem, dev):
        return pltpu.make_async_remote_copy(
            src_ref=src, dst_ref=dst, send_sem=ssem, recv_sem=rsem, device_id=dev, device_id_type=MESH
        )

    def push(*what):
        cp = remote(*what)
        cp.start()
        sent.append(cp)

    own_rows.wait()
    split = (NEAR + 1) // 2
    spans = ((0, split), (split, NEAR - split))
    axes = ((ag_a, x, x_dev), (ag_b, y, y_dev))

    def piece(h, o, s, core):
        buf, pos, _ = axes[h]
        return buf.at[pl.ds((turn(pos, o) * CORES + core) * NEAR + spans[s][0], spans[s][1])]

    def share(h, o, s):
        push(piece(h, o, s, c), piece(h, o, s, c), core_send.at[h, o, s], core_recv.at[h, o, s], twin)

    for h in range(2):
        buf, pos, devs = axes[h]
        base = (pos * CORES + c) * NEAR

        def reblock(d, carry, h=h, buf=buf, base=base):
            col = pl.multiple_of(lax.rem(sn + d, BLOCKS) * width, width)
            buf[base + d] = rows[h * half:(h + 1) * half, pl.ds(col, width)]
            return carry

        lax.fori_loop(0, NEAR, reblock, 0)
        for order in range(2):
            for e in range(2):
                s = (order, 1 - order)[e]
                push(piece(h, 0, s, c), piece(h, 0, s, c), ring_send.at[h, e, s], ring_recv.at[h, e, s], devs[step[e]])
        for s in range(2):
            share(h, 0, s)

    for cp in loads:
        cp.wait()
    inv_one, inv_two = parts(loaded[1]), parts(loaded[3])
    u_all[z, 0] = mul(parts(loaded[0]), inv_one)
    u_all[z, 1] = mul(parts(loaded[2]), inv_two)

    def u_part(o, n):
        return u_all.at[turn(z, o), n]

    for order in range(2):
        for e in range(2):
            n = (order, 1 - order)[e]
            push(u_part(0, n), u_part(0, n), pan_send.at[e, n], pan_recv.at[e, n], z_dev[step[e]])

    def fill(n, carry):
        o = lax.rem(n, SIDE)
        along_x = n // SIDE
        item = at(turn(x, o * along_x), turn(y, o * (1 - along_x)), c)
        for p, (i, k) in enumerate(PAIRS):
            row, dist, swap = locate(structure[item, i], structure[item, k])
            rx, ry, rc = place(row)
            table[n, p] = (jnp.where(along_x == 0, rx, ry) * CORES + rc) * NEAR + dist
            table[n, NP + p] = jnp.where(along_x == 0, ry, rx)
            table[n, 2 * NP + p] = swap.astype(jnp.int32)
        return carry

    lax.fori_loop(0, 2 * SIDE, fill, 0)

    def ring_wait(h, e, s):
        o = (BELOW, ABOVE)[e]
        remote(piece(h, o, s, c), piece(h, o, s, c), ring_send.at[h, e, s], ring_recv.at[h, e, s], axes[h][2][step[e]]).wait_recv()
        return o

    for h in range(2):
        for e in range(2):
            o = ring_wait(h, e, e)
            push(piece(h, o, e, c), piece(h, o, e, c), fwd_send.at[h, e], fwd_recv.at[h, e], axes[h][2][step[e]])
            share(h, o, e)
    def split_u(o):
        for n in range(2):
            at_k = turn(z, o)
            u_high[at_k, :, n * width:(n + 1) * width], u_low[at_k, :, n * width:(n + 1) * width] = parts(u_all[at_k, n])

    u_par = mul(parts(loaded[4]), inv_two)
    par[...] = u_par
    for e in range(2):
        o = (BELOW, ABOVE)[e]
        remote(u_part(o, e), u_part(o, e), pan_send.at[e, e], pan_recv.at[e, e], z_dev[step[e]]).wait_recv()
        push(u_part(o, e), u_part(o, e), pan_fsend.at[e], pan_frecv.at[e], z_dev[step[e]])
    split_u(0)
    for h in range(2):
        for e in range(2):
            share(h, ring_wait(h, e, 1 - e), 1 - e)
    diag_one[...] = mul(inv_one, inv_one, 0, 0)
    rest_two[...] = mul(inv_two, inv_two, 0, 0)
    for h in range(2):
        for e in range(2):
            remote(piece(h, 2, e, c), piece(h, 2, e, c), fwd_send.at[h, e], fwd_recv.at[h, e], axes[h][2][step[e]]).wait_recv()
            share(h, 2, e)

    for h in range(2):
        for o in (0, BELOW, ABOVE, 2):
            for s in range(2):
                remote(piece(h, o, s, 1 - c), piece(h, o, s, 1 - c), core_send.at[h, o, s], core_recv.at[h, o, s], twin).wait_recv()
    routes = ((ag_a, y, y_dev), (ag_b, x, x_dev))

    def pick(h, o, p):
        return routes[h][0][table[h * SIDE + o, p]]

    def owner(h, o, p):
        return table[h * SIDE + o, NP + p]

    half_pairs = NP // 2
    for h in range(2):
        devs = routes[h][2]
        for g in range(half_pairs):
            for e in range(2):
                relay_out[h, e, g] = pick(h, 2, 2 * g + e)
                push(
                    relay_out.at[h, e, g], relay_in.at[h, e, g],
                    relay_send.at[h, e, g], relay_recv.at[h, e, g], devs[step[e]],
                )
    for h in range(2):
        for p in range(NP):
            own_in[h, p] = pick(h, 0, p)
    for g in range(half_pairs):
        for h in range(2):
            pos, devs = routes[h][1], routes[h][2]
            for e in range(2):
                o = step[e]
                remote(
                    relay_out.at[h, e, g], relay_in.at[h, e, g],
                    relay_send.at[h, e, g], relay_recv.at[h, e, g], devs[o],
                ).wait_recv()
                for q in range(2):
                    p = 2 * g + q
                    value = pick(h, o, p)
                    if q == e:
                        value = jnp.where(owner(h, o, p) == turn(pos, SIDE - o), relay_in[h, e, g], value)
                    main_out[h, e, p] = value
                push(
                    main_out.at[h, e, pl.ds(2 * g, 2)], main_in.at[h, e, pl.ds(2 * g, 2)],
                    main_send.at[h, e, g], main_recv.at[h, e, g], devs[o],
                )

    def zpart(o, lo, n):
        return zed.at[pl.ds(turn(z, o) * NP + lo, n)]

    def gather(g):
        for h in range(2):
            pos, devs = routes[h][1], routes[h][2]
            for e in range(2):
                remote(
                    main_out.at[h, e, pl.ds(2 * g, 2)], main_in.at[h, e, pl.ds(2 * g, 2)],
                    main_send.at[h, e, g], main_recv.at[h, e, g], devs[step[e]],
                ).wait_recv()
            for q in range(2):
                p = 2 * g + q
                who = owner(h, 0, p)
                below, above = main_in[h, UP, p], main_in[h, DOWN, p]
                far = below if q == UP else above
                value = jnp.where(who == pos, own_in[h, p], far)
                value = jnp.where(who == turn(pos, BELOW), below, value)
                value = jnp.where(who == turn(pos, ABOVE), above, value)
                zed[z * NP + p, h * half:(h + 1) * half] = value
        for e in range(2):
            push(zpart(0, 2 * g, 2), zpart(0, 2 * g, 2), z_send.at[e, g], z_recv.at[e, g], z_dev[step[e]])

    def hand_on(g):
        for e in range(2):
            o = (BELOW, ABOVE)[e]
            remote(zpart(o, 2 * g, 2), zpart(o, 2 * g, 2), z_send.at[e, g], z_recv.at[e, g], z_dev[step[e]]).wait_recv()
            push(zpart(o, 2 * g + e, 1), zpart(o, 2 * g + e, 1), zf_send.at[e, g], zf_recv.at[e, g], z_dev[step[e]])

    def arrive(g):
        for e in range(2):
            remote(zpart(2, 2 * g + e, 1), zpart(2, 2 * g + e, 1), zf_send.at[e, g], zf_recv.at[e, g], z_dev[step[e]]).wait_recv()

    def products(p):
        i, k = PAIRS[p]
        block = jnp.concatenate([zed[q * NP + p] for q in range(SIDE)], axis=0)
        flipped = block.T
        swap = table[0, 2 * NP + p] == 1
        direct = parts(jnp.where(swap, flipped, block))
        value = mul(direct, (u_high[k], u_low[k]))
        w[i] = value if i == 0 and k == 0 else w[i] + value
        if i != k:
            value = mul(parts(jnp.where(swap, block, flipped)), (u_high[i], u_low[i]))
            w[k] = value if i == 0 else w[k] + value
        if k == POSITIONS - 1:
            one = (u_high[i, :, :width], u_low[i, :, :width])
            two = (u_high[i, :, width:], u_low[i, :, width:])
            w_one, w_two = parts(w[i, :, :width]), parts(w[i, :, width:])
            diag_one[...] += mul(one, w_one, 0, 0)
            cross = mul(two, w_one, 0, 0)
            mixed[...] = cross if i == 0 else mixed[...] + cross
            rest_two[...] += mul(two, w_two, 0, 0)

    for e in range(2):
        n, o = 1 - e, (BELOW, ABOVE)[e]
        remote(u_part(o, n), u_part(o, n), pan_send.at[e, n], pan_recv.at[e, n], z_dev[step[e]]).wait_recv()
        remote(u_part(2, e), u_part(2, e), pan_fsend.at[e], pan_frecv.at[e], z_dev[step[e]]).wait_recv()
    for o in range(1, SIDE):
        split_u(o)
    for t in range(half_pairs + 2):
        if t < half_pairs:
            gather(t)
        if 1 <= t <= half_pairs:
            hand_on(t - 1)
        if t >= 2:
            arrive(t - 2)
            for q in range(2):
                products(2 * (t - 2) + q)
    own_w[...] = w[z]
    for cp in sent:
        cp.wait_send()


def exchange(structure, root, panel_one, panel_two, inverse_one, parent, inverse_two):
    width = panel_one.shape[0]
    quarter, half = width // SIDE, width // SIDE // 2
    f32 = jnp.float32
    dma = pltpu.SemaphoreType.DMA
    hbm = pl.BlockSpec(memory_space=pltpu.HBM)
    vmem = pl.BlockSpec(memory_space=pltpu.VMEM)
    groups = NP // 2
    square = jax.ShapeDtypeStruct((width, width), f32)
    return pl.pallas_call(
        exchange_kernel,
        out_shape=(jax.ShapeDtypeStruct((width, 2 * width), f32),) + (square,) * 4,
        in_specs=[pl.BlockSpec(memory_space=pltpu.SMEM)] + [hbm] * 6,
        out_specs=(vmem,) * 5,
        scratch_shapes=[
            pltpu.VMEM((SIDE * NP, quarter, width), f32),
            pltpu.VMEM((5, width, width), f32),
            pltpu.VMEM((POSITIONS, 2, width, width), f32),
            pltpu.VMEM((POSITIONS, width, 2 * width), jnp.bfloat16),
            pltpu.VMEM((POSITIONS, width, 2 * width), jnp.bfloat16),
            pltpu.VMEM((POSITIONS, width, 2 * width), f32),
            pltpu.SMEM((2 * SIDE, 3 * NP), jnp.int32),
            pltpu.VMEM((quarter, root.shape[1]), f32),
            pltpu.VMEM((SIDE * CORES * NEAR, half, width), f32),
            pltpu.VMEM((SIDE * CORES * NEAR, half, width), f32),
            pltpu.VMEM((2, 2, NP, half, width), f32),
            pltpu.VMEM((2, 2, NP, half, width), f32),
            pltpu.VMEM((2, NP, half, width), f32),
            pltpu.VMEM((2, 2, groups, half, width), f32),
            pltpu.VMEM((2, 2, groups, half, width), f32),
            dma,
            dma((5,)),
            dma((2, 2)), dma((2, 2)), dma((2,)), dma((2,)),
            dma((2, 2, 2)), dma((2, 2, 2)), dma((2, 2)), dma((2, 2)),
            dma((2, SIDE, 2)), dma((2, SIDE, 2)),
            dma((2, 2, groups)), dma((2, 2, groups)),
            dma((2, 2, groups)), dma((2, 2, groups)),
            dma((2, groups)), dma((2, groups)), dma((2, groups)), dma((2, groups)),
        ],
        compiler_params=pltpu.CompilerParams(
            collective_id=0, has_side_effects=True, vmem_limit_bytes=57 * 2**20
        ),
        name="exchange",
    )(structure, root, panel_one, panel_two, inverse_one, parent, inverse_two)


def finish_kernel(w, total_one, mixed, rest_two, par, diag_one, off_one, diag_two, par_two, root_two):
    width = par.shape[0]
    u_par = parts(par[...])
    w_one = w[:, :width]
    diag_one[...] = total_one[...]
    off_one[...] = -w_one
    root_two[...] = mul(parts(w_one), u_par) - w[:, width:]
    cross = mixed[...]
    p_two = cross.T - mul(parts(total_one[...]), u_par)
    par_two[...] = p_two
    diag_two[...] = rest_two[...] - mul(parts(cross), u_par) - mul(u_par, parts(p_two), 0, 0)


def finish(*args):
    vmem = pl.BlockSpec(memory_space=pltpu.VMEM)
    return pl.pallas_call(
        finish_kernel,
        out_shape=(jax.ShapeDtypeStruct(args[-1].shape, jnp.float32),) * 5,
        in_specs=[vmem] * 5,
        out_specs=(vmem,) * 5,
        compiler_params=pltpu.CompilerParams(vmem_limit_bytes=16 * 2**20),
        name="finish",
    )(*args)


def per_device(root_inverse, structure, panel_one, inverse_one, parent_two, panel_two, inverse_two):
    sums = exchange(
        structure, root_inverse, panel_one[0], panel_two[0], inverse_one[0], parent_two[0], inverse_two[0]
    )
    return tuple(out[None] for out in finish(*sums))


def solution(mesh):
    return jax.shard_map(
        per_device,
        mesh=mesh,
        in_specs=(
            P("sn", None),
            P(),
            P("sn", "blk", None),
            P("sn", None, None),
            P("sn", None, None),
            P("sn", "blk", None),
            P("sn", None, None),
        ),
        out_specs=(
            P("sn", None, None),
            P("sn", "blk", None),
            P("sn", None, None),
            P("sn", None, None),
            P("sn", "blk", None),
        ),
        check_vma=False,
    )
```

```python
import functools

import jax
import jax.numpy as jnp
from jax import lax
from jax.experimental import pallas as pl
from jax.experimental.pallas import tpu as pltpu
from jax.sharding import PartitionSpec as P

MESH = pl.DeviceIdType.MESH
SIDE = 4
CORES = 2
POSITIONS = 4
PAIRS = tuple((i, k) for i in range(POSITIONS) for k in range(i, POSITIONS))
NP = len(PAIRS)
BLOCKS = 32
PARTS = 2
GROUPS = ((0, 2), (2, 2), (4, 2), (6, 2), (8, 2))
NEAR = BLOCKS // 2 + 1


def locate(a, b):
    d = jnp.bitwise_and(b - a + BLOCKS, BLOCKS - 1)
    swap = d >= NEAR
    return jnp.where(swap, b, a), jnp.where(swap, BLOCKS - d, d), swap


def parts(v):
    high = v.astype(jnp.bfloat16)
    return high, (v - high.astype(jnp.float32)).astype(jnp.bfloat16)


def mul(a, b, ca=1, cb=0):
    dims = (((ca,), (cb,)), ((), ()))
    dot = functools.partial(lax.dot_general, dimension_numbers=dims, preferred_element_type=jnp.float32)
    return dot(a[0], b[0]) + (dot(a[0], b[1]) + dot(a[1], b[0]))


def place(row):
    return row // (SIDE * CORES), lax.rem(row // CORES, SIDE), lax.rem(row, CORES)


def exchange_kernel(
    structure, root, panel_one, panel_two, inverse_one, parent, inverse_two,
    own_w, diag_one, mixed, rest_two, par,
    zed, loaded, u_all, u_high, u_low, w, table, rows,
    ag_00, ag_01, ag_10, ag_11, main_out, main_in, own_in,
    root_sem, load_sem, pan_send, pan_recv, pan_fsend, pan_frecv,
    ring_send, ring_recv, fwd_send, fwd_recv, core_send, core_recv,
    main_send, main_recv, z_send, z_recv, zf_send, zf_recv,
):
    width = panel_one.shape[0]
    quarter = width // SIDE
    part = quarter // PARTS
    half = part // 2
    sn = lax.axis_index("sn")
    z = lax.axis_index("blk")
    x, y, c = place(sn)
    ag = ((ag_00, ag_01), (ag_10, ag_11))

    def at(xx, yy, cc):
        return (xx * SIDE + yy) * CORES + cc

    def turn(v, o):
        return lax.rem(v + o, SIDE)

    x_dev = [(at(turn(x, o), y, c), z) for o in range(SIDE)]
    y_dev = [(at(x, turn(y, o), c), z) for o in range(SIDE)]
    z_dev = [(sn, turn(z, o)) for o in range(SIDE)]
    twin = (at(x, y, 1 - c), z)
    BELOW, ABOVE = 3, 1
    step = (1, 3)

    own_rows = [
        pltpu.make_async_copy(
            root.at[pl.ds(pl.multiple_of(z * quarter + r * 8, 8), 8), :], rows.at[pl.ds(r * 8, 8)], root_sem.at[r]
        )
        for r in range(quarter // 8)
    ]
    for cp in own_rows:
        cp.start()
    loads = [
        pltpu.make_async_copy(src, loaded.at[n], load_sem.at[n])
        for n, src in enumerate((panel_one, inverse_one, panel_two, inverse_two, parent))
    ]
    for cp in loads:
        cp.start()

    barrier = pltpu.get_barrier_semaphore()
    partners = x_dev[1:] + y_dev[1:] + [z_dev[1], z_dev[3], twin]
    for dev in partners:
        pl.semaphore_signal(barrier, inc=1, device_id=dev, device_id_type=MESH)
    pl.semaphore_wait(barrier, len(partners))

    sent = []

    def remote(src, dst, ssem, rsem, dev):
        return pltpu.make_async_remote_copy(
            src_ref=src, dst_ref=dst, send_sem=ssem, recv_sem=rsem, device_id=dev, device_id_type=MESH
        )

    def push(*what):
        cp = remote(*what)
        cp.start()
        sent.append(cp)

    split = (NEAR + 1) // 2
    spans = ((0, split), (split, NEAR - split))
    axes = ((x, x_dev), (y, y_dev))

    def piece(v, h, o, s, core):
        return ag[v][h].at[pl.ds((turn(axes[h][0], o) * CORES + core) * NEAR + spans[s][0], spans[s][1])]

    def ring(v, h, e, s, o):
        return remote(piece(v, h, o, s, c), piece(v, h, o, s, c), ring_send.at[v, h, e, s], ring_recv.at[v, h, e, s], axes[h][1][step[e]])

    def forward(v, h, e, o):
        return remote(piece(v, h, o, e, c), piece(v, h, o, e, c), fwd_send.at[v, h, e], fwd_recv.at[v, h, e], axes[h][1][step[e]])

    def twins(v, h, o, s, core):
        return remote(piece(v, h, o, s, core), piece(v, h, o, s, core), core_send.at[v, h, o, s], core_recv.at[v, h, o, s], twin)

    def go(cp):
        cp.start()
        sent.append(cp)

    def reblock(v, h):
        base = (axes[h][0] * CORES + c) * NEAR
        top = v * part + h * half

        def one(d, carry):
            col = pl.multiple_of(lax.rem(sn + d, BLOCKS) * width, width)
            ag[v][h][base + d] = rows[top:top + half, pl.ds(col, width)]
            return carry

        lax.fori_loop(0, NEAR, one, 0)

    def own_out(v, h):
        for order in range(2):
            for e in range(2):
                go(ring(v, h, e, (order, 1 - order)[e], 0))
        for s in range(2):
            go(twins(v, h, 0, s, c))

    def first_in(v, h):
        for e in range(2):
            o = (BELOW, ABOVE)[e]
            ring(v, h, e, e, o).wait_recv()
            go(forward(v, h, e, o))
            go(twins(v, h, o, e, c))

    def second_in(v, h):
        for e in range(2):
            o = (BELOW, ABOVE)[e]
            ring(v, h, e, 1 - e, o).wait_recv()
            go(twins(v, h, o, 1 - e, c))

    def far_in(v, h):
        for e in range(2):
            forward(v, h, e, 2).wait_recv()
            go(twins(v, h, 2, e, c))

    def twins_in(v, h):
        for o in (0, BELOW, ABOVE, 2):
            for s in range(2):
                twins(v, h, o, s, 1 - c).wait_recv()

    routes = ((y, y_dev), (x, x_dev))

    def listed(v, h, o, g):
        lo, n = GROUPS[g]
        return remote(
            main_out.at[v, h, o - 1, pl.ds(lo, n)], main_in.at[v, h, o - 1, pl.ds(lo, n)],
            main_send.at[v, h, o - 1, g], main_recv.at[v, h, o - 1, g], routes[h][1][o],
        )

    def listed_out(v, g):
        lo, n = GROUPS[g]
        for o in (2, 1, 3):
            for h in range(2):
                for p in range(lo, lo + n):
                    main_out[v, h, o - 1, p] = ag[v][h][table[h * SIDE + o, p]]
                listed(v, h, o, g).start()
        for h in range(2):
            for p in range(lo, lo + n):
                own_in[v, h, p] = ag[v][h][table[h * SIDE, p]]

    def listed_sent(v, g):
        for o in range(1, SIDE):
            for h in range(2):
                listed(v, h, o, g).wait_send()

    def zpart(v, o, lo, n):
        return zed.at[pl.ds((v * SIDE + turn(z, o)) * NP + lo, n)]

    def z_copy(v, o, e, g):
        lo, n = GROUPS[g]
        return remote(zpart(v, o, lo, n), zpart(v, o, lo, n), z_send.at[v, e, g], z_recv.at[v, e, g], z_dev[step[e]])

    def z_forward(v, o, e, g):
        lo, n = GROUPS[g]
        return remote(
            zpart(v, o, lo + e * (n // 2), n // 2), zpart(v, o, lo + e * (n // 2), n // 2),
            zf_send.at[v, e, g], zf_recv.at[v, e, g], z_dev[step[e]],
        )

    def listed_in(v, g):
        lo, n = GROUPS[g]
        for h in range(2):
            pos = routes[h][0]
            for o in range(1, SIDE):
                listed(v, h, o, g).wait_recv()
            for p in range(lo, lo + n):
                who = table[h * SIDE, NP + p]
                value = own_in[v, h, p]
                for o in range(1, SIDE):
                    value = jnp.where(who == turn(pos, SIDE - o), main_in[v, h, o - 1, p], value)
                zed[(v * SIDE + z) * NP + p, h * half:(h + 1) * half] = value
        for e in range(2):
            go(z_copy(v, 0, e, g))

    def hand_on(v, g):
        for e in range(2):
            o = (BELOW, ABOVE)[e]
            z_copy(v, o, e, g).wait_recv()
            go(z_forward(v, o, e, g))

    def arrive(v, g):
        for e in range(2):
            z_forward(v, 2, e, g).wait_recv()

    def u_part(o, n):
        return u_all.at[turn(z, o), n]

    def u_copy(o, e, n):
        return remote(u_part(o, n), u_part(o, n), pan_send.at[e, n], pan_recv.at[e, n], z_dev[step[e]])

    def u_forward(o, e):
        return remote(u_part(o, e), u_part(o, e), pan_fsend.at[e], pan_frecv.at[e], z_dev[step[e]])

    def split_u(o):
        for n in range(2):
            at_k = turn(z, o)
            u_high[at_k, :, n * width:(n + 1) * width], u_low[at_k, :, n * width:(n + 1) * width] = parts(u_all[at_k, n])

    def fill(n, carry):
        o = lax.rem(n, SIDE)
        along_x = n // SIDE
        item = at(turn(x, o * along_x), turn(y, o * (1 - along_x)), c)
        for p, (i, k) in enumerate(PAIRS):
            row, dist, swap = locate(structure[i, item], structure[k, item])
            rx, ry, rc = place(row)
            table[n, p] = (jnp.where(along_x == 0, rx, ry) * CORES + rc) * NEAR + dist
            table[n, NP + p] = jnp.where(along_x == 0, ry, rx)
            table[n, 2 * NP + p] = swap.astype(jnp.int32)
        return carry

    def products(p):
        i, k = PAIRS[p]
        block = jnp.concatenate(
            [zed[(v * SIDE + q) * NP + p] for q in range(SIDE) for v in range(PARTS)], axis=0
        )
        flipped = block.T
        swap = table[0, 2 * NP + p] == 1
        direct = parts(jnp.where(swap, flipped, block))
        value = mul(direct, (u_high[k], u_low[k]))
        w[i] = value if i == 0 and k == 0 else w[i] + value
        if i != k:
            value = mul(parts(jnp.where(swap, block, flipped)), (u_high[i], u_low[i]))
            w[k] = value if i == 0 else w[k] + value
        if k == POSITIONS - 1:
            one = (u_high[i, :, :width], u_low[i, :, :width])
            two = (u_high[i, :, width:], u_low[i, :, width:])
            w_one, w_two = parts(w[i, :, :width]), parts(w[i, :, width:])
            diag_one[...] += mul(one, w_one, 0, 0)
            cross = mul(two, w_one, 0, 0)
            mixed[...] = cross if i == 0 else mixed[...] + cross
            rest_two[...] += mul(two, w_two, 0, 0)

    count = len(GROUPS)
    for cp in own_rows[:part // 8]:
        cp.wait()
    for h in range(2):
        reblock(0, h)
        own_out(0, h)
    for cp in loads:
        cp.wait()
    inv_one, inv_two = parts(loaded[1]), parts(loaded[3])
    u_all[z, 0] = mul(parts(loaded[0]), inv_one)
    u_all[z, 1] = mul(parts(loaded[2]), inv_two)
    for order in range(2):
        for e in range(2):
            go(u_copy(0, e, (order, 1 - order)[e]))
    for cp in own_rows[part // 8:]:
        cp.wait()
    for h in range(2):
        reblock(1, h)
    lax.fori_loop(0, 2 * SIDE, fill, 0)
    for h in range(2):
        first_in(0, h)
    for h in range(2):
        second_in(0, h)
    for h in range(2):
        own_out(1, h)
    for e in range(2):
        o = (BELOW, ABOVE)[e]
        u_copy(o, e, e).wait_recv()
        go(u_forward(o, e))
    for h in range(2):
        far_in(0, h)
    par[...] = mul(parts(loaded[4]), inv_two)
    for h in range(2):
        twins_in(0, h)
    listed_out(0, 0)
    listed_out(0, 1)
    diag_one[...] = mul(inv_one, inv_one, 0, 0)
    rest_two[...] = mul(inv_two, inv_two, 0, 0)
    for h in range(2):
        first_in(1, h)
    listed_sent(0, 0)
    listed_out(0, 2)
    listed_in(0, 0)
    for h in range(2):
        second_in(1, h)
    listed_sent(0, 1)
    listed_out(0, 3)
    listed_in(0, 1)
    listed_sent(0, 2)
    listed_out(0, 4)
    split_u(0)
    for h in range(2):
        far_in(1, h)
    listed_in(0, 2)
    for h in range(2):
        twins_in(1, h)
    listed_out(1, 0)
    listed_out(1, 1)
    hand_on(0, 0)
    listed_in(0, 3)
    listed_in(0, 4)
    hand_on(0, 1)
    for e in range(2):
        u_copy((BELOW, ABOVE)[e], e, 1 - e).wait_recv()
        u_forward(2, e).wait_recv()
    for t in range(count + 2):
        if t + 2 < count:
            listed_sent(1, t)
            listed_out(1, t + 2)
            hand_on(0, t + 2)
        if t < count:
            listed_in(1, t)
        if t == 0:
            split_u(1)
            split_u(2)
        if 1 <= t <= count:
            hand_on(1, t - 1)
        if t >= 2:
            arrive(0, t - 2)
            arrive(1, t - 2)
            lo, n = GROUPS[t - 2]
            if t == 2:
                split_u(3)
            for p in range(lo, lo + n):
                products(p)
    for v, g in ((0, 3), (0, 4), (1, 3), (1, 4)):
        listed_sent(v, g)
    own_w[...] = w[z]
    for cp in sent:
        cp.wait_send()


def exchange(structure, root, panel_one, panel_two, inverse_one, parent, inverse_two):
    width = panel_one.shape[0]
    quarter = width // SIDE
    part = quarter // PARTS
    half = part // 2
    f32 = jnp.float32
    dma = pltpu.SemaphoreType.DMA
    hbm = pl.BlockSpec(memory_space=pltpu.HBM)
    vmem = pl.BlockSpec(memory_space=pltpu.VMEM)
    groups = len(GROUPS)
    square = jax.ShapeDtypeStruct((width, width), f32)
    gathered = pltpu.VMEM((SIDE * CORES * NEAR, half, width), f32)
    return pl.pallas_call(
        exchange_kernel,
        out_shape=(jax.ShapeDtypeStruct((width, 2 * width), f32),) + (square,) * 4,
        in_specs=[pl.BlockSpec(memory_space=pltpu.SMEM)] + [hbm] * 6,
        out_specs=(vmem,) * 5,
        scratch_shapes=[
            pltpu.VMEM((PARTS * SIDE * NP, part, width), f32),
            pltpu.VMEM((5, width, width), f32),
            pltpu.VMEM((POSITIONS, 2, width, width), f32),
            pltpu.VMEM((POSITIONS, width, 2 * width), jnp.bfloat16),
            pltpu.VMEM((POSITIONS, width, 2 * width), jnp.bfloat16),
            pltpu.VMEM((POSITIONS, width, 2 * width), f32),
            pltpu.SMEM((2 * SIDE, 3 * NP), jnp.int32),
            pltpu.VMEM((quarter, root.shape[1]), f32),
            gathered, gathered, gathered, gathered,
            pltpu.VMEM((PARTS, 2, SIDE - 1, NP, half, width), f32),
            pltpu.VMEM((PARTS, 2, SIDE - 1, NP, half, width), f32),
            pltpu.VMEM((PARTS, 2, NP, half, width), f32),
            dma((quarter // 8,)),
            dma((5,)),
            dma((2, 2)), dma((2, 2)), dma((2,)), dma((2,)),
            dma((PARTS, 2, 2, 2)), dma((PARTS, 2, 2, 2)), dma((PARTS, 2, 2)), dma((PARTS, 2, 2)),
            dma((PARTS, 2, SIDE, 2)), dma((PARTS, 2, SIDE, 2)),
            dma((PARTS, 2, SIDE - 1, groups)), dma((PARTS, 2, SIDE - 1, groups)),
            dma((PARTS, 2, groups)), dma((PARTS, 2, groups)), dma((PARTS, 2, groups)), dma((PARTS, 2, groups)),
        ],
        compiler_params=pltpu.CompilerParams(
            collective_id=0, has_side_effects=True, vmem_limit_bytes=57 * 2**20
        ),
        name="exchange",
    )(structure, root, panel_one, panel_two, inverse_one, parent, inverse_two)


def finish_kernel(w, total_one, mixed, rest_two, par, diag_one, off_one, diag_two, par_two, root_two):
    width = par.shape[0]
    u_par = parts(par[...])
    w_one = w[:, :width]
    diag_one[...] = total_one[...]
    off_one[...] = -w_one
    root_two[...] = mul(parts(w_one), u_par) - w[:, width:]
    cross = mixed[...]
    p_two = cross.T - mul(parts(total_one[...]), u_par)
    par_two[...] = p_two
    diag_two[...] = rest_two[...] - mul(parts(cross), u_par) - mul(u_par, parts(p_two), 0, 0)


def finish(*args):
    vmem = pl.BlockSpec(memory_space=pltpu.VMEM)
    return pl.pallas_call(
        finish_kernel,
        out_shape=(jax.ShapeDtypeStruct(args[-1].shape, jnp.float32),) * 5,
        in_specs=[vmem] * 5,
        out_specs=(vmem,) * 5,
        compiler_params=pltpu.CompilerParams(vmem_limit_bytes=60 * 2**20),
        name="finish",
    )(*args)


def per_device(root_inverse, structure, panel_one, inverse_one, parent_two, panel_two, inverse_two):
    sums = exchange(
        structure.T, root_inverse, panel_one[0], panel_two[0], inverse_one[0], parent_two[0], inverse_two[0]
    )
    return tuple(out[None] for out in finish(*sums))


def solution(mesh):
    return jax.shard_map(
        per_device,
        mesh=mesh,
        in_specs=(
            P("sn", None),
            P(),
            P("sn", "blk", None),
            P("sn", None, None),
            P("sn", None, None),
            P("sn", "blk", None),
            P("sn", None, None),
        ),
        out_specs=(
            P("sn", None, None),
            P("sn", "blk", None),
            P("sn", None, None),
            P("sn", None, None),
            P("sn", "blk", None),
        ),
        check_vma=False,
    )
```

```python
import functools

import jax
import jax.numpy as jnp
from jax import lax
from jax.experimental import pallas as pl
from jax.experimental.pallas import tpu as pltpu
from jax.sharding import PartitionSpec as P

MESH = pl.DeviceIdType.MESH
SIDE = 4
CORES = 2
POSITIONS = 4
PAIRS = tuple((i, k) for i in range(POSITIONS) for k in range(i, POSITIONS))
NP = len(PAIRS)
BLOCKS = 32
PARTS = 2
GROUPS = ((0, 4), (4, 4), (8, 2))
NEAR = BLOCKS // 2 + 1


SEQUENCE = (
    ("F", 0), ("S", 0), ("O", 1), ("U",), ("R", 0), ("Q",), ("T", 0), ("L", 0, 0),
    ("L", 0, 1), ("L", 0, 2), ("D",), ("F", 1), ("I", 0, 0), ("S", 1), ("I", 0, 1), ("H", 0, 0),
    ("R", 1), ("I", 0, 2), ("H", 0, 1), ("X", 0), ("T", 1), ("L", 1, 0), ("L", 1, 1), ("L", 1, 2),
    ("H", 0, 2), ("V",), ("I", 1, 0), ("X", 1), ("X", 2), ("I", 1, 1), ("H", 1, 0), ("I", 1, 2),
    ("H", 1, 1), ("A", 0, 0), ("A", 1, 0), ("X", 3), ("P", 0), ("H", 1, 2), ("A", 0, 1), ("A", 1, 1),
    ("P", 1), ("A", 0, 2), ("A", 1, 2), ("P", 2),
)


def locate(a, b):
    d = jnp.bitwise_and(b - a + BLOCKS, BLOCKS - 1)
    swap = d >= NEAR
    return jnp.where(swap, b, a), jnp.where(swap, BLOCKS - d, d), swap


def parts(v):
    high = v.astype(jnp.bfloat16)
    return high, (v - high.astype(jnp.float32)).astype(jnp.bfloat16)


def mul(a, b, ca=1, cb=0):
    dims = (((ca,), (cb,)), ((), ()))
    left = jnp.concatenate([a[0], a[0], a[1]], axis=ca)
    right = jnp.concatenate([b[0], b[1], b[0]], axis=cb)
    return lax.dot_general(left, right, dimension_numbers=dims, preferred_element_type=jnp.float32)


def place(row):
    return row // (SIDE * CORES), lax.rem(row // CORES, SIDE), lax.rem(row, CORES)


def exchange_kernel(
    structure, root, panel_one, panel_two, inverse_one, parent, inverse_two,
    own_w, diag_one, mixed, rest_two, par,
    zed, loaded, u_all, u_high, u_low, w, table, rows,
    ag_00, ag_01, ag_10, ag_11, main_out, main_in, own_in,
    root_sem, load_sem, pan_send, pan_recv, pan_fsend, pan_frecv,
    ring_send, ring_recv, fwd_send, fwd_recv, core_send, core_recv,
    main_send, main_recv, z_send, z_recv, zf_send, zf_recv,
):
    width = panel_one.shape[0]
    quarter = width // SIDE
    part = quarter // PARTS
    half = part // 2
    sn = lax.axis_index("sn")
    z = lax.axis_index("blk")
    x, y, c = place(sn)
    ag = ((ag_00, ag_01), (ag_10, ag_11))

    def at(xx, yy, cc):
        return (xx * SIDE + yy) * CORES + cc

    def turn(v, o):
        return lax.rem(v + o, SIDE)

    x_dev = [(at(turn(x, o), y, c), z) for o in range(SIDE)]
    y_dev = [(at(x, turn(y, o), c), z) for o in range(SIDE)]
    z_dev = [(sn, turn(z, o)) for o in range(SIDE)]
    twin = (at(x, y, 1 - c), z)
    BELOW, ABOVE = 3, 1
    step = (1, 3)

    own_rows = [
        pltpu.make_async_copy(
            root.at[pl.ds(pl.multiple_of(z * quarter + r * 8, 8), 8), :], rows.at[pl.ds(r * 8, 8)], root_sem.at[r]
        )
        for r in range(quarter // 8)
    ]
    for cp in own_rows:
        cp.start()
    loads = [
        pltpu.make_async_copy(src, loaded.at[n], load_sem.at[n])
        for n, src in enumerate((panel_one, inverse_one, panel_two, inverse_two, parent))
    ]
    for cp in loads:
        cp.start()

    barrier = pltpu.get_barrier_semaphore()
    partners = x_dev[1:] + y_dev[1:] + [z_dev[1], z_dev[3], twin]
    for dev in partners:
        pl.semaphore_signal(barrier, inc=1, device_id=dev, device_id_type=MESH)
    pl.semaphore_wait(barrier, len(partners))

    sent = []

    def remote(src, dst, ssem, rsem, dev):
        return pltpu.make_async_remote_copy(
            src_ref=src, dst_ref=dst, send_sem=ssem, recv_sem=rsem, device_id=dev, device_id_type=MESH
        )

    def push(*what):
        cp = remote(*what)
        cp.start()
        sent.append(cp)

    split = (NEAR + 1) // 2
    spans = ((0, split), (split, NEAR - split))
    axes = ((x, x_dev), (y, y_dev))

    def piece(v, h, o, s, core):
        return ag[v][h].at[pl.ds((turn(axes[h][0], o) * CORES + core) * NEAR + spans[s][0], spans[s][1])]

    def ring(v, h, e, s, o):
        return remote(piece(v, h, o, s, c), piece(v, h, o, s, c), ring_send.at[v, h, e, s], ring_recv.at[v, h, e, s], axes[h][1][step[e]])

    def forward(v, h, e, o):
        return remote(piece(v, h, o, e, c), piece(v, h, o, e, c), fwd_send.at[v, h, e], fwd_recv.at[v, h, e], axes[h][1][step[e]])

    def twins(v, h, o, s, core):
        return remote(piece(v, h, o, s, core), piece(v, h, o, s, core), core_send.at[v, h, o, s], core_recv.at[v, h, o, s], twin)

    def go(cp):
        cp.start()
        sent.append(cp)

    def reblock(v, h):
        base = (axes[h][0] * CORES + c) * NEAR
        top = v * part + h * half

        def one(d, carry):
            col = pl.multiple_of(lax.rem(sn + d, BLOCKS) * width, width)
            ag[v][h][base + d] = rows[top:top + half, pl.ds(col, width)]
            return carry

        lax.fori_loop(0, NEAR, one, 0)

    def own_out(v, h):
        for order in range(2):
            for e in range(2):
                go(ring(v, h, e, (order, 1 - order)[e], 0))
        for s in range(2):
            go(twins(v, h, 0, s, c))

    def first_in(v, h):
        for e in range(2):
            o = (BELOW, ABOVE)[e]
            ring(v, h, e, e, o).wait_recv()
            go(forward(v, h, e, o))
            go(twins(v, h, o, e, c))

    def second_in(v, h):
        for e in range(2):
            o = (BELOW, ABOVE)[e]
            ring(v, h, e, 1 - e, o).wait_recv()
            go(twins(v, h, o, 1 - e, c))

    def far_in(v, h):
        for e in range(2):
            forward(v, h, e, 2).wait_recv()
            go(twins(v, h, 2, e, c))

    def twins_in(v, h):
        for o in (0, BELOW, ABOVE, 2):
            for s in range(2):
                twins(v, h, o, s, 1 - c).wait_recv()

    routes = ((y, y_dev), (x, x_dev))

    def listed(v, h, o, g):
        lo, n = GROUPS[g]
        return remote(
            main_out.at[v, h, o - 1, pl.ds(lo, n)], main_in.at[v, h, o - 1, pl.ds(lo, n)],
            main_send.at[v, h, o - 1, g], main_recv.at[v, h, o - 1, g], routes[h][1][o],
        )

    def listed_out(v, g):
        lo, n = GROUPS[g]
        for o in (2, 1, 3):
            for h in range(2):
                for p in range(lo, lo + n):
                    main_out[v, h, o - 1, p] = ag[v][h][table[h * SIDE + o, p]]
                listed(v, h, o, g).start()
        for h in range(2):
            for p in range(lo, lo + n):
                own_in[v, h, p] = ag[v][h][table[h * SIDE, p]]

    def listed_sent(v, g):
        for o in range(1, SIDE):
            for h in range(2):
                listed(v, h, o, g).wait_send()

    def zpart(v, o, lo, n):
        return zed.at[pl.ds((v * SIDE + turn(z, o)) * NP + lo, n)]

    def z_copy(v, o, e, g):
        lo, n = GROUPS[g]
        return remote(zpart(v, o, lo, n), zpart(v, o, lo, n), z_send.at[v, e, g], z_recv.at[v, e, g], z_dev[step[e]])

    def z_forward(v, o, e, g):
        lo, n = GROUPS[g]
        return remote(
            zpart(v, o, lo + e * (n // 2), n // 2), zpart(v, o, lo + e * (n // 2), n // 2),
            zf_send.at[v, e, g], zf_recv.at[v, e, g], z_dev[step[e]],
        )

    def listed_in(v, g):
        lo, n = GROUPS[g]
        for h in range(2):
            pos = routes[h][0]
            for o in range(1, SIDE):
                listed(v, h, o, g).wait_recv()
            for p in range(lo, lo + n):
                who = table[h * SIDE, NP + p]
                value = own_in[v, h, p]
                for o in range(1, SIDE):
                    value = jnp.where(who == turn(pos, SIDE - o), main_in[v, h, o - 1, p], value)
                zed[(v * SIDE + z) * NP + p, h * half:(h + 1) * half] = value
        for e in range(2):
            go(z_copy(v, 0, e, g))

    def hand_on(v, g):
        for e in range(2):
            o = (BELOW, ABOVE)[e]
            z_copy(v, o, e, g).wait_recv()
            go(z_forward(v, o, e, g))

    def arrive(v, g):
        for e in range(2):
            z_forward(v, 2, e, g).wait_recv()

    def u_part(o, n):
        return u_all.at[turn(z, o), n]

    def u_copy(o, e, n):
        return remote(u_part(o, n), u_part(o, n), pan_send.at[e, n], pan_recv.at[e, n], z_dev[step[e]])

    def u_forward(o, e):
        return remote(u_part(o, e), u_part(o, e), pan_fsend.at[e], pan_frecv.at[e], z_dev[step[e]])

    def split_u(o):
        for n in range(2):
            at_k = turn(z, o)
            u_high[at_k, :, n * width:(n + 1) * width], u_low[at_k, :, n * width:(n + 1) * width] = parts(u_all[at_k, n])

    def fill(n, carry):
        o = lax.rem(n, SIDE)
        along_x = n // SIDE
        item = at(turn(x, o * along_x), turn(y, o * (1 - along_x)), c)
        for p, (i, k) in enumerate(PAIRS):
            row, dist, swap = locate(structure[i, item], structure[k, item])
            rx, ry, rc = place(row)
            table[n, p] = (jnp.where(along_x == 0, rx, ry) * CORES + rc) * NEAR + dist
            table[n, NP + p] = jnp.where(along_x == 0, ry, rx)
            table[n, 2 * NP + p] = swap.astype(jnp.int32)
        return carry

    def products(p):
        i, k = PAIRS[p]
        block = jnp.concatenate(
            [zed[(v * SIDE + q) * NP + p] for q in range(SIDE) for v in range(PARTS)], axis=0
        )
        flipped = block.T
        swap = table[0, 2 * NP + p] == 1
        direct = parts(jnp.where(swap, flipped, block))
        value = mul(direct, (u_high[k], u_low[k]))
        w[i] = value if i == 0 and k == 0 else w[i] + value
        if i != k:
            value = mul(parts(jnp.where(swap, block, flipped)), (u_high[i], u_low[i]))
            w[k] = value if i == 0 else w[k] + value
        if k == POSITIONS - 1:
            one = (u_high[i, :, :width], u_low[i, :, :width])
            two = (u_high[i, :, width:], u_low[i, :, width:])
            w_one, w_two = parts(w[i, :, :width]), parts(w[i, :, width:])
            diag_one[...] += mul(one, w_one, 0, 0)
            cross = mul(two, w_one, 0, 0)
            mixed[...] = cross if i == 0 else mixed[...] + cross
            rest_two[...] += mul(two, w_two, 0, 0)

    for cp in own_rows[:part // 8]:
        cp.wait()
    for h in range(2):
        reblock(0, h)
        own_out(0, h)
    for cp in loads:
        cp.wait()
    inv_one, inv_two = parts(loaded[1]), parts(loaded[3])
    u_all[z, 0] = mul(parts(loaded[0]), inv_one)
    u_all[z, 1] = mul(parts(loaded[2]), inv_two)
    for order in range(2):
        for e in range(2):
            go(u_copy(0, e, (order, 1 - order)[e]))
    for cp in own_rows[part // 8:]:
        cp.wait()
    for h in range(2):
        reblock(1, h)
    lax.fori_loop(0, 2 * SIDE, fill, 0)
    def both(f):
        def run(v):
            for h in range(2):
                f(v, h)

        return run

    def u_on():
        for e in range(2):
            o = (BELOW, ABOVE)[e]
            u_copy(o, e, e).wait_recv()
            go(u_forward(o, e))

    def u_in():
        for e in range(2):
            u_copy((BELOW, ABOVE)[e], e, 1 - e).wait_recv()
            u_forward(2, e).wait_recv()

    def squares():
        diag_one[...] = mul(inv_one, inv_one, 0, 0)
        rest_two[...] = mul(inv_two, inv_two, 0, 0)

    def u_parent():
        par[...] = mul(parts(loaded[4]), inv_two)

    def multiply(g):
        lo, n = GROUPS[g]
        for p in range(lo, lo + n):
            products(p)

    steps = {
        "O": both(own_out), "F": both(first_in), "S": both(second_in), "R": both(far_in), "T": both(twins_in),
        "L": listed_out, "K": listed_sent, "I": listed_in, "H": hand_on, "A": arrive, "P": multiply,
        "U": u_on, "V": u_in, "D": squares, "Q": u_parent, "X": split_u,
    }
    for name, *at_what in SEQUENCE:
        steps[name](*at_what)
    for v in range(PARTS):
        for g in range(len(GROUPS)):
            if ("K", v, g) not in SEQUENCE:
                listed_sent(v, g)
    own_w[...] = w[z]
    for cp in sent:
        cp.wait_send()


def exchange(structure, root, panel_one, panel_two, inverse_one, parent, inverse_two):
    width = panel_one.shape[0]
    quarter = width // SIDE
    part = quarter // PARTS
    half = part // 2
    f32 = jnp.float32
    dma = pltpu.SemaphoreType.DMA
    hbm = pl.BlockSpec(memory_space=pltpu.HBM)
    vmem = pl.BlockSpec(memory_space=pltpu.VMEM)
    groups = len(GROUPS)
    square = jax.ShapeDtypeStruct((width, width), f32)
    gathered = pltpu.VMEM((SIDE * CORES * NEAR, half, width), f32)
    return pl.pallas_call(
        exchange_kernel,
        out_shape=(jax.ShapeDtypeStruct((width, 2 * width), f32),) + (square,) * 4,
        in_specs=[pl.BlockSpec(memory_space=pltpu.SMEM)] + [hbm] * 6,
        out_specs=(vmem,) * 5,
        scratch_shapes=[
            pltpu.VMEM((PARTS * SIDE * NP, part, width), f32),
            pltpu.VMEM((5, width, width), f32),
            pltpu.VMEM((POSITIONS, 2, width, width), f32),
            pltpu.VMEM((POSITIONS, width, 2 * width), jnp.bfloat16),
            pltpu.VMEM((POSITIONS, width, 2 * width), jnp.bfloat16),
            pltpu.VMEM((POSITIONS, width, 2 * width), f32),
            pltpu.SMEM((2 * SIDE, 3 * NP), jnp.int32),
            pltpu.VMEM((quarter, root.shape[1]), f32),
            gathered, gathered, gathered, gathered,
            pltpu.VMEM((PARTS, 2, SIDE - 1, NP, half, width), f32),
            pltpu.VMEM((PARTS, 2, SIDE - 1, NP, half, width), f32),
            pltpu.VMEM((PARTS, 2, NP, half, width), f32),
            dma((quarter // 8,)),
            dma((5,)),
            dma((2, 2)), dma((2, 2)), dma((2,)), dma((2,)),
            dma((PARTS, 2, 2, 2)), dma((PARTS, 2, 2, 2)), dma((PARTS, 2, 2)), dma((PARTS, 2, 2)),
            dma((PARTS, 2, SIDE, 2)), dma((PARTS, 2, SIDE, 2)),
            dma((PARTS, 2, SIDE - 1, groups)), dma((PARTS, 2, SIDE - 1, groups)),
            dma((PARTS, 2, groups)), dma((PARTS, 2, groups)), dma((PARTS, 2, groups)), dma((PARTS, 2, groups)),
        ],
        compiler_params=pltpu.CompilerParams(
            collective_id=0, has_side_effects=True, vmem_limit_bytes=57 * 2**20
        ),
        name="exchange",
    )(structure, root, panel_one, panel_two, inverse_one, parent, inverse_two)


def finish_kernel(w, total_one, mixed, rest_two, par, diag_one, off_one, diag_two, par_two, root_two):
    width = par.shape[0]
    u_par = parts(par[...])
    w_one = w[:, :width]
    diag_one[...] = total_one[...]
    off_one[...] = -w_one
    root_two[...] = mul(parts(w_one), u_par) - w[:, width:]
    cross = mixed[...]
    p_two = cross.T - mul(parts(total_one[...]), u_par)
    par_two[...] = p_two
    diag_two[...] = rest_two[...] - mul(parts(cross), u_par) - mul(u_par, parts(p_two), 0, 0)


def finish(*args):
    vmem = pl.BlockSpec(memory_space=pltpu.VMEM)
    return pl.pallas_call(
        finish_kernel,
        out_shape=(jax.ShapeDtypeStruct(args[-1].shape, jnp.float32),) * 5,
        in_specs=[vmem] * 5,
        out_specs=(vmem,) * 5,
        compiler_params=pltpu.CompilerParams(vmem_limit_bytes=60 * 2**20),
        name="finish",
    )(*args)


def per_device(root_inverse, structure, panel_one, inverse_one, parent_two, panel_two, inverse_two):
    sums = exchange(
        structure.T, root_inverse, panel_one[0], panel_two[0], inverse_one[0], parent_two[0], inverse_two[0]
    )
    return tuple(out[None] for out in finish(*sums))


def solution(mesh):
    return jax.shard_map(
        per_device,
        mesh=mesh,
        in_specs=(
            P("sn", None),
            P(),
            P("sn", "blk", None),
            P("sn", None, None),
            P("sn", None, None),
            P("sn", "blk", None),
            P("sn", None, None),
        ),
        out_specs=(
            P("sn", None, None),
            P("sn", "blk", None),
            P("sn", None, None),
            P("sn", None, None),
            P("sn", "blk", None),
        ),
        check_vma=False,
    )
```

```python
import functools

import jax
import jax.numpy as jnp
from jax import lax
from jax.experimental import pallas as pl
from jax.experimental.pallas import tpu as pltpu
from jax.sharding import PartitionSpec as P

MESH = pl.DeviceIdType.MESH
SIDE = 4
CORES = 2
POSITIONS = 4
PAIRS = tuple((i, k) for i in range(POSITIONS) for k in range(i, POSITIONS))
NP = len(PAIRS)
BLOCKS = 32
PARTS = 2
GROUPS = ((0, 2), (2, 2), (4, 2), (6, 2), (8, 2))
NEAR = BLOCKS // 2 + 1


SEQUENCE = (
    ("F", 0), ("S", 0), ("O", 1), ("U",), ("R", 0), ("Q",), ("T", 0), ("L", 0, 0),
    ("L", 0, 1), ("K", 0, 0), ("L", 0, 2), ("D",), ("F", 1), ("I", 0, 0), ("K", 0, 1), ("L", 0, 3),
    ("I", 0, 1), ("H", 0, 0), ("S", 1), ("K", 0, 2), ("L", 0, 4), ("I", 0, 2), ("H", 0, 1), ("R", 1),
    ("I", 0, 3), ("H", 0, 2), ("T", 1), ("L", 1, 0), ("L", 1, 1), ("I", 0, 4), ("H", 0, 3), ("V",),
    ("H", 0, 4), ("K", 1, 0), ("L", 1, 2), ("X", 0), ("I", 1, 0), ("K", 1, 1), ("L", 1, 3), ("X", 1),
    ("I", 1, 1), ("H", 1, 0), ("K", 1, 2), ("L", 1, 4), ("X", 2), ("I", 1, 2), ("H", 1, 1), ("X", 3),
    ("I", 1, 3), ("H", 1, 2), ("A", 0, 0), ("A", 1, 0), ("P", 0), ("I", 1, 4), ("H", 1, 3), ("A", 0, 1),
    ("A", 1, 1), ("P", 1), ("H", 1, 4), ("A", 0, 2), ("A", 1, 2), ("P", 2), ("A", 0, 3), ("A", 1, 3),
    ("P", 3), ("A", 0, 4), ("A", 1, 4), ("P", 4),
)


def locate(a, b):
    d = jnp.bitwise_and(b - a + BLOCKS, BLOCKS - 1)
    swap = d >= NEAR
    return jnp.where(swap, b, a), jnp.where(swap, BLOCKS - d, d), swap


def parts(v):
    high = v.astype(jnp.bfloat16)
    return high, (v - high.astype(jnp.float32)).astype(jnp.bfloat16)


def mul(a, b, ca=1, cb=0):
    dims = (((ca,), (cb,)), ((), ()))
    left = jnp.concatenate([a[0], a[0], a[1]], axis=ca)
    right = jnp.concatenate([b[0], b[1], b[0]], axis=cb)
    return lax.dot_general(left, right, dimension_numbers=dims, preferred_element_type=jnp.float32)


def place(row):
    return row // (SIDE * CORES), lax.rem(row // CORES, SIDE), lax.rem(row, CORES)


def exchange_kernel(
    structure, root, panel_one, panel_two, inverse_one, parent, inverse_two,
    own_w, diag_one, mixed, rest_two, par,
    zed, loaded, u_all, u_high, u_low, w, table, rows,
    ag_00, ag_01, ag_10, ag_11, main_out, main_in, own_in,
    root_sem, load_sem, pan_send, pan_recv, pan_fsend, pan_frecv,
    ring_send, ring_recv, fwd_send, fwd_recv, core_send, core_recv,
    main_send, main_recv, z_send, z_recv, zf_send, zf_recv,
):
    width = panel_one.shape[0]
    quarter = width // SIDE
    part = quarter // PARTS
    half = part // 2
    sn = lax.axis_index("sn")
    z = lax.axis_index("blk")
    x, y, c = place(sn)
    ag = ((ag_00, ag_01), (ag_10, ag_11))

    def at(xx, yy, cc):
        return (xx * SIDE + yy) * CORES + cc

    def turn(v, o):
        return lax.rem(v + o, SIDE)

    x_dev = [(at(turn(x, o), y, c), z) for o in range(SIDE)]
    y_dev = [(at(x, turn(y, o), c), z) for o in range(SIDE)]
    z_dev = [(sn, turn(z, o)) for o in range(SIDE)]
    twin = (at(x, y, 1 - c), z)
    BELOW, ABOVE = 3, 1
    step = (1, 3)

    barrier = pltpu.get_barrier_semaphore()
    partners = x_dev[1:] + y_dev[1:] + [z_dev[1], z_dev[3], twin]
    for dev in partners:
        pl.semaphore_signal(barrier, inc=1, device_id=dev, device_id_type=MESH)
    own_rows = [
        pltpu.make_async_copy(
            root.at[pl.ds(pl.multiple_of(z * quarter + r * 8, 8), 8), :], rows.at[pl.ds(r * 8, 8)], root_sem.at[r]
        )
        for r in range(quarter // 8)
    ]
    for cp in own_rows:
        cp.start()
    loads = [
        pltpu.make_async_copy(src, loaded.at[n], load_sem.at[n])
        for n, src in enumerate((panel_one, inverse_one, panel_two, inverse_two, parent))
    ]
    for cp in loads:
        cp.start()
    pl.semaphore_wait(barrier, len(partners))

    sent = []

    def remote(src, dst, ssem, rsem, dev):
        return pltpu.make_async_remote_copy(
            src_ref=src, dst_ref=dst, send_sem=ssem, recv_sem=rsem, device_id=dev, device_id_type=MESH
        )

    def push(*what):
        cp = remote(*what)
        cp.start()
        sent.append(cp)

    split = (NEAR + 1) // 2
    spans = ((0, split), (split, NEAR - split))
    axes = ((x, x_dev), (y, y_dev))

    def piece(v, h, o, s, core):
        return ag[v][h].at[pl.ds((turn(axes[h][0], o) * CORES + core) * NEAR + spans[s][0], spans[s][1])]

    def ring(v, h, e, s, o):
        return remote(piece(v, h, o, s, c), piece(v, h, o, s, c), ring_send.at[v, h, e, s], ring_recv.at[v, h, e, s], axes[h][1][step[e]])

    def forward(v, h, e, o):
        return remote(piece(v, h, o, e, c), piece(v, h, o, e, c), fwd_send.at[v, h, e], fwd_recv.at[v, h, e], axes[h][1][step[e]])

    def twins(v, h, o, s, core):
        return remote(piece(v, h, o, s, core), piece(v, h, o, s, core), core_send.at[v, h, o, s], core_recv.at[v, h, o, s], twin)

    def go(cp):
        cp.start()
        sent.append(cp)

    def reblock(v, h):
        base = (axes[h][0] * CORES + c) * NEAR
        top = v * part + h * half

        def one(d, carry):
            col = pl.multiple_of(lax.rem(sn + d, BLOCKS) * width, width)
            ag[v][h][base + d] = rows[top:top + half, pl.ds(col, width)]
            return carry

        lax.fori_loop(0, NEAR, one, 0)

    def own_out(v, h):
        for order in range(2):
            for e in range(2):
                go(ring(v, h, e, (order, 1 - order)[e], 0))
        for s in range(2):
            go(twins(v, h, 0, s, c))

    def first_in(v, h):
        for e in range(2):
            o = (BELOW, ABOVE)[e]
            ring(v, h, e, e, o).wait_recv()
            go(forward(v, h, e, o))
            go(twins(v, h, o, e, c))

    def second_in(v, h):
        for e in range(2):
            o = (BELOW, ABOVE)[e]
            ring(v, h, e, 1 - e, o).wait_recv()
            go(twins(v, h, o, 1 - e, c))

    def far_in(v, h):
        for e in range(2):
            forward(v, h, e, 2).wait_recv()
            go(twins(v, h, 2, e, c))

    def twins_in(v, h):
        for o in (0, BELOW, ABOVE, 2):
            for s in range(2):
                twins(v, h, o, s, 1 - c).wait_recv()

    routes = ((y, y_dev), (x, x_dev))

    def listed(v, h, o, g):
        lo, n = GROUPS[g]
        return remote(
            main_out.at[v, h, o - 1, pl.ds(lo, n)], main_in.at[v, h, o - 1, pl.ds(lo, n)],
            main_send.at[v, h, o - 1, g], main_recv.at[v, h, o - 1, g], routes[h][1][o],
        )

    def listed_out(v, g):
        lo, n = GROUPS[g]
        for o in (2, 1, 3):
            for h in range(2):
                for p in range(lo, lo + n):
                    main_out[v, h, o - 1, p] = ag[v][h][table[h * SIDE + o, p]]
                listed(v, h, o, g).start()
        for h in range(2):
            for p in range(lo, lo + n):
                own_in[v, h, p] = ag[v][h][table[h * SIDE, p]]

    def listed_sent(v, g):
        for o in range(1, SIDE):
            for h in range(2):
                listed(v, h, o, g).wait_send()

    def zpart(v, o, lo, n):
        return zed.at[pl.ds((v * SIDE + turn(z, o)) * NP + lo, n)]

    def z_copy(v, o, e, g):
        lo, n = GROUPS[g]
        return remote(zpart(v, o, lo, n), zpart(v, o, lo, n), z_send.at[v, e, g], z_recv.at[v, e, g], z_dev[step[e]])

    def z_forward(v, o, e, g):
        lo, n = GROUPS[g]
        return remote(
            zpart(v, o, lo + e * (n // 2), n // 2), zpart(v, o, lo + e * (n // 2), n // 2),
            zf_send.at[v, e, g], zf_recv.at[v, e, g], z_dev[step[e]],
        )

    def listed_in(v, g):
        lo, n = GROUPS[g]
        for h in range(2):
            pos = routes[h][0]
            for o in range(1, SIDE):
                listed(v, h, o, g).wait_recv()
            for p in range(lo, lo + n):
                who = table[h * SIDE, NP + p]
                value = own_in[v, h, p]
                for o in range(1, SIDE):
                    value = jnp.where(who == turn(pos, SIDE - o), main_in[v, h, o - 1, p], value)
                zed[(v * SIDE + z) * NP + p, h * half:(h + 1) * half] = value
        for e in range(2):
            go(z_copy(v, 0, e, g))

    def hand_on(v, g):
        for e in range(2):
            o = (BELOW, ABOVE)[e]
            z_copy(v, o, e, g).wait_recv()
            go(z_forward(v, o, e, g))

    def arrive(v, g):
        for e in range(2):
            z_forward(v, 2, e, g).wait_recv()

    def u_part(o, n):
        return u_all.at[turn(z, o), n]

    def u_copy(o, e, n):
        return remote(u_part(o, n), u_part(o, n), pan_send.at[e, n], pan_recv.at[e, n], z_dev[step[e]])

    def u_forward(o, e):
        return remote(u_part(o, e), u_part(o, e), pan_fsend.at[e], pan_frecv.at[e], z_dev[step[e]])

    def split_u(o):
        for n in range(2):
            at_k = turn(z, o)
            u_high[at_k, :, n * width:(n + 1) * width], u_low[at_k, :, n * width:(n + 1) * width] = parts(u_all[at_k, n])

    def fill(n, carry):
        o = lax.rem(n, SIDE)
        along_x = n // SIDE
        item = at(turn(x, o * along_x), turn(y, o * (1 - along_x)), c)
        for p, (i, k) in enumerate(PAIRS):
            row, dist, swap = locate(structure[i, item], structure[k, item])
            rx, ry, rc = place(row)
            table[n, p] = (jnp.where(along_x == 0, rx, ry) * CORES + rc) * NEAR + dist
            table[n, NP + p] = jnp.where(along_x == 0, ry, rx)
            table[n, 2 * NP + p] = swap.astype(jnp.int32)
        return carry

    def products(p):
        i, k = PAIRS[p]
        block = jnp.concatenate(
            [zed[(v * SIDE + q) * NP + p] for q in range(SIDE) for v in range(PARTS)], axis=0
        )
        flipped = block.T
        swap = table[0, 2 * NP + p] == 1
        direct = parts(jnp.where(swap, flipped, block))
        value = mul(direct, (u_high[k], u_low[k]))
        w[i] = value if i == 0 and k == 0 else w[i] + value
        if i != k:
            value = mul(parts(jnp.where(swap, block, flipped)), (u_high[i], u_low[i]))
            w[k] = value if i == 0 else w[k] + value
        if k == POSITIONS - 1:
            one = (u_high[i, :, :width], u_low[i, :, :width])
            two = (u_high[i, :, width:], u_low[i, :, width:])
            w_one, w_two = parts(w[i, :, :width]), parts(w[i, :, width:])
            diag_one[...] += mul(one, w_one, 0, 0)
            cross = mul(two, w_one, 0, 0)
            mixed[...] = cross if i == 0 else mixed[...] + cross
            rest_two[...] += mul(two, w_two, 0, 0)

    for cp in own_rows[:part // 8]:
        cp.wait()
    for h in range(2):
        reblock(0, h)
        own_out(0, h)
    for cp in loads:
        cp.wait()
    inv_one, inv_two = parts(loaded[1]), parts(loaded[3])
    u_all[z, 0] = mul(parts(loaded[0]), inv_one)
    u_all[z, 1] = mul(parts(loaded[2]), inv_two)
    for order in range(2):
        for e in range(2):
            go(u_copy(0, e, (order, 1 - order)[e]))
    for cp in own_rows[part // 8:]:
        cp.wait()
    for h in range(2):
        reblock(1, h)
    lax.fori_loop(0, 2 * SIDE, fill, 0)
    def both(f):
        def run(v):
            for h in range(2):
                f(v, h)

        return run

    def u_on():
        for e in range(2):
            o = (BELOW, ABOVE)[e]
            u_copy(o, e, e).wait_recv()
            go(u_forward(o, e))

    def u_in():
        for e in range(2):
            u_copy((BELOW, ABOVE)[e], e, 1 - e).wait_recv()
            u_forward(2, e).wait_recv()

    def squares():
        diag_one[...] = mul(inv_one, inv_one, 0, 0)
        rest_two[...] = mul(inv_two, inv_two, 0, 0)

    def u_parent():
        par[...] = mul(parts(loaded[4]), inv_two)

    def multiply(g):
        lo, n = GROUPS[g]
        for p in range(lo, lo + n):
            products(p)

    steps = {
        "O": both(own_out), "F": both(first_in), "S": both(second_in), "R": both(far_in), "T": both(twins_in),
        "L": listed_out, "K": listed_sent, "I": listed_in, "H": hand_on, "A": arrive, "P": multiply,
        "U": u_on, "V": u_in, "D": squares, "Q": u_parent, "X": split_u,
    }
    for name, *at_what in SEQUENCE:
        steps[name](*at_what)
    for v in range(PARTS):
        for g in range(len(GROUPS)):
            if ("K", v, g) not in SEQUENCE:
                listed_sent(v, g)
    own_w[...] = w[z]
    for cp in sent:
        cp.wait_send()


def exchange(structure, root, panel_one, panel_two, inverse_one, parent, inverse_two):
    width = panel_one.shape[0]
    quarter = width // SIDE
    part = quarter // PARTS
    half = part // 2
    f32 = jnp.float32
    dma = pltpu.SemaphoreType.DMA
    hbm = pl.BlockSpec(memory_space=pltpu.HBM)
    vmem = pl.BlockSpec(memory_space=pltpu.VMEM)
    groups = len(GROUPS)
    square = jax.ShapeDtypeStruct((width, width), f32)
    gathered = pltpu.VMEM((SIDE * CORES * NEAR, half, width), f32)
    return pl.pallas_call(
        exchange_kernel,
        out_shape=(jax.ShapeDtypeStruct((width, 2 * width), f32),) + (square,) * 4,
        in_specs=[pl.BlockSpec(memory_space=pltpu.SMEM)] + [hbm] * 6,
        out_specs=(vmem,) * 5,
        scratch_shapes=[
            pltpu.VMEM((PARTS * SIDE * NP, part, width), f32),
            pltpu.VMEM((5, width, width), f32),
            pltpu.VMEM((POSITIONS, 2, width, width), f32),
            pltpu.VMEM((POSITIONS, width, 2 * width), jnp.bfloat16),
            pltpu.VMEM((POSITIONS, width, 2 * width), jnp.bfloat16),
            pltpu.VMEM((POSITIONS, width, 2 * width), f32),
            pltpu.SMEM((2 * SIDE, 3 * NP), jnp.int32),
            pltpu.VMEM((quarter, root.shape[1]), f32),
            gathered, gathered, gathered, gathered,
            pltpu.VMEM((PARTS, 2, SIDE - 1, NP, half, width), f32),
            pltpu.VMEM((PARTS, 2, SIDE - 1, NP, half, width), f32),
            pltpu.VMEM((PARTS, 2, NP, half, width), f32),
            dma((quarter // 8,)),
            dma((5,)),
            dma((2, 2)), dma((2, 2)), dma((2,)), dma((2,)),
            dma((PARTS, 2, 2, 2)), dma((PARTS, 2, 2, 2)), dma((PARTS, 2, 2)), dma((PARTS, 2, 2)),
            dma((PARTS, 2, SIDE, 2)), dma((PARTS, 2, SIDE, 2)),
            dma((PARTS, 2, SIDE - 1, groups)), dma((PARTS, 2, SIDE - 1, groups)),
            dma((PARTS, 2, groups)), dma((PARTS, 2, groups)), dma((PARTS, 2, groups)), dma((PARTS, 2, groups)),
        ],
        compiler_params=pltpu.CompilerParams(
            collective_id=0, has_side_effects=True, vmem_limit_bytes=57 * 2**20
        ),
        name="exchange",
    )(structure, root, panel_one, panel_two, inverse_one, parent, inverse_two)


def finish_kernel(w, total_one, mixed, rest_two, par, diag_one, off_one, diag_two, par_two, root_two):
    width = par.shape[0]
    u_par = parts(par[...])
    w_one = w[:, :width]
    diag_one[...] = total_one[...]
    off_one[...] = -w_one
    root_two[...] = mul(parts(w_one), u_par) - w[:, width:]
    cross = mixed[...]
    p_two = cross.T - mul(parts(total_one[...]), u_par)
    par_two[...] = p_two
    diag_two[...] = rest_two[...] - mul(parts(cross), u_par) - mul(u_par, parts(p_two), 0, 0)


def finish(*args):
    vmem = pl.BlockSpec(memory_space=pltpu.VMEM)
    return pl.pallas_call(
        finish_kernel,
        out_shape=(jax.ShapeDtypeStruct(args[-1].shape, jnp.float32),) * 5,
        in_specs=[vmem] * 5,
        out_specs=(vmem,) * 5,
        compiler_params=pltpu.CompilerParams(vmem_limit_bytes=60 * 2**20),
        name="finish",
    )(*args)


def per_device(root_inverse, structure, panel_one, inverse_one, parent_two, panel_two, inverse_two):
    sums = exchange(
        structure.T, root_inverse, panel_one[0], panel_two[0], inverse_one[0], parent_two[0], inverse_two[0]
    )
    return tuple(out[None] for out in finish(*sums))


def solution(mesh):
    return jax.shard_map(
        per_device,
        mesh=mesh,
        in_specs=(
            P("sn", None),
            P(),
            P("sn", "blk", None),
            P("sn", None, None),
            P("sn", None, None),
            P("sn", "blk", None),
            P("sn", None, None),
        ),
        out_specs=(
            P("sn", None, None),
            P("sn", "blk", None),
            P("sn", None, None),
            P("sn", None, None),
            P("sn", "blk", None),
        ),
        check_vma=False,
    )
```

```python
import functools

import jax
import jax.numpy as jnp
from jax import lax
from jax.experimental import pallas as pl
from jax.experimental.pallas import tpu as pltpu
from jax.sharding import PartitionSpec as P

MESH = pl.DeviceIdType.MESH
SIDE = 4
CORES = 2
POSITIONS = 4
PAIRS = tuple((i, k) for i in range(POSITIONS) for k in range(i, POSITIONS))
NP = len(PAIRS)
BLOCKS = 32
PARTS = 2
DIRECT = ((1, 2),)
GROUPS = ((0, 4), (4, 4), (8, 2))
NEAR = BLOCKS // 2 + 1


SEQUENCE = (
    ("F", 0), ("S", 0), ("O", 1), ("U",), ("R", 0), ("Q",), ("T", 0), ("L", 0, 0),
    ("L", 0, 1), ("L", 0, 2), ("D",), ("F", 1), ("I", 0, 0), ("S", 1), ("I", 0, 1), ("H", 0, 0),
    ("R", 1), ("I", 0, 2), ("H", 0, 1), ("X", 0), ("T", 1), ("L", 1, 0), ("L", 1, 1), ("L", 1, 2),
    ("H", 0, 2), ("V",), ("I", 1, 0), ("X", 1), ("X", 2), ("I", 1, 1), ("H", 1, 0), ("I", 1, 2),
    ("H", 1, 1), ("A", 0, 0), ("A", 1, 0), ("X", 3), ("P", 0), ("H", 1, 2), ("A", 0, 1), ("A", 1, 1),
    ("P", 1), ("A", 0, 2), ("A", 1, 2), ("P", 2),
)


def locate(a, b):
    d = jnp.bitwise_and(b - a + BLOCKS, BLOCKS - 1)
    swap = d >= NEAR
    return jnp.where(swap, b, a), jnp.where(swap, BLOCKS - d, d), swap


def parts(v):
    high = v.astype(jnp.bfloat16)
    return high, (v - high.astype(jnp.float32)).astype(jnp.bfloat16)


def mul(a, b, ca=1, cb=0):
    dims = (((ca,), (cb,)), ((), ()))
    left = jnp.concatenate([a[0], a[0], a[1]], axis=ca)
    right = jnp.concatenate([b[0], b[1], b[0]], axis=cb)
    return lax.dot_general(left, right, dimension_numbers=dims, preferred_element_type=jnp.float32)


def place(row):
    return row // (SIDE * CORES), lax.rem(row // CORES, SIDE), lax.rem(row, CORES)


def exchange_kernel(
    structure, root, panel_one, panel_two, inverse_one, parent, inverse_two,
    own_w, diag_one, mixed, rest_two, par,
    zed, loaded, u_all, u_high, u_low, w, table, rows,
    ag_00, ag_01, ag_10, ag_11, main_out, main_in, own_in,
    root_sem, load_sem, pan_send, pan_recv, pan_fsend, pan_frecv,
    ring_send, ring_recv, fwd_send, fwd_recv, core_send, core_recv,
    main_send, main_recv, z_send, z_recv, zf_send, zf_recv,
):
    width = panel_one.shape[0]
    quarter = width // SIDE
    part = quarter // PARTS
    half = part // 2
    sn = lax.axis_index("sn")
    z = lax.axis_index("blk")
    x, y, c = place(sn)
    ag = ((ag_00, ag_01), (ag_10, ag_11))

    def at(xx, yy, cc):
        return (xx * SIDE + yy) * CORES + cc

    def turn(v, o):
        return lax.rem(v + o, SIDE)

    x_dev = [(at(turn(x, o), y, c), z) for o in range(SIDE)]
    y_dev = [(at(x, turn(y, o), c), z) for o in range(SIDE)]
    z_dev = [(sn, turn(z, o)) for o in range(SIDE)]
    twin = (at(x, y, 1 - c), z)
    BELOW, ABOVE = 3, 1
    step = (1, 3)

    own_rows = [
        pltpu.make_async_copy(
            root.at[pl.ds(pl.multiple_of(z * quarter + r * 8, 8), 8), :], rows.at[pl.ds(r * 8, 8)], root_sem.at[r]
        )
        for r in range(quarter // 8)
    ]
    for cp in own_rows:
        cp.start()
    loads = [
        pltpu.make_async_copy(src, loaded.at[n], load_sem.at[n])
        for n, src in enumerate((panel_one, inverse_one, panel_two, inverse_two, parent))
    ]
    for cp in loads:
        cp.start()

    barrier = pltpu.get_barrier_semaphore()
    partners = x_dev[1:] + y_dev[1:] + z_dev[1:] + [twin]
    for dev in partners:
        pl.semaphore_signal(barrier, inc=1, device_id=dev, device_id_type=MESH)
    pl.semaphore_wait(barrier, len(partners))

    sent = []

    def remote(src, dst, ssem, rsem, dev):
        return pltpu.make_async_remote_copy(
            src_ref=src, dst_ref=dst, send_sem=ssem, recv_sem=rsem, device_id=dev, device_id_type=MESH
        )

    def push(*what):
        cp = remote(*what)
        cp.start()
        sent.append(cp)

    split = (NEAR + 1) // 2
    spans = ((0, split), (split, NEAR - split))
    axes = ((x, x_dev), (y, y_dev))

    def piece(v, h, o, s, core):
        return ag[v][h].at[pl.ds((turn(axes[h][0], o) * CORES + core) * NEAR + spans[s][0], spans[s][1])]

    def ring(v, h, e, s, o):
        return remote(piece(v, h, o, s, c), piece(v, h, o, s, c), ring_send.at[v, h, e, s], ring_recv.at[v, h, e, s], axes[h][1][step[e]])

    def forward(v, h, e, o):
        return remote(piece(v, h, o, e, c), piece(v, h, o, e, c), fwd_send.at[v, h, e], fwd_recv.at[v, h, e], axes[h][1][step[e]])

    def twins(v, h, o, s, core):
        return remote(piece(v, h, o, s, core), piece(v, h, o, s, core), core_send.at[v, h, o, s], core_recv.at[v, h, o, s], twin)

    def go(cp):
        cp.start()
        sent.append(cp)

    def reblock(v, h):
        base = (axes[h][0] * CORES + c) * NEAR
        top = v * part + h * half

        def one(d, carry):
            col = pl.multiple_of(lax.rem(sn + d, BLOCKS) * width, width)
            ag[v][h][base + d] = rows[top:top + half, pl.ds(col, width)]
            return carry

        lax.fori_loop(0, NEAR, one, 0)

    def own_out(v, h):
        for order in range(2):
            for e in range(2):
                go(ring(v, h, e, (order, 1 - order)[e], 0))
        for s in range(2):
            go(twins(v, h, 0, s, c))

    def first_in(v, h):
        for e in range(2):
            o = (BELOW, ABOVE)[e]
            ring(v, h, e, e, o).wait_recv()
            go(forward(v, h, e, o))
            go(twins(v, h, o, e, c))

    def second_in(v, h):
        for e in range(2):
            o = (BELOW, ABOVE)[e]
            ring(v, h, e, 1 - e, o).wait_recv()
            go(twins(v, h, o, 1 - e, c))

    def far_in(v, h):
        for e in range(2):
            forward(v, h, e, 2).wait_recv()
            go(twins(v, h, 2, e, c))

    def twins_in(v, h):
        for o in (0, BELOW, ABOVE, 2):
            for s in range(2):
                twins(v, h, o, s, 1 - c).wait_recv()

    routes = ((y, y_dev), (x, x_dev))

    def listed(v, h, o, g):
        lo, n = GROUPS[g]
        return remote(
            main_out.at[v, h, o - 1, pl.ds(lo, n)], main_in.at[v, h, o - 1, pl.ds(lo, n)],
            main_send.at[v, h, o - 1, g], main_recv.at[v, h, o - 1, g], routes[h][1][o],
        )

    def listed_out(v, g):
        lo, n = GROUPS[g]
        for o in (2, 1, 3):
            for h in range(2):
                for p in range(lo, lo + n):
                    main_out[v, h, o - 1, p] = ag[v][h][table[h * SIDE + o, p]]
                listed(v, h, o, g).start()
        for h in range(2):
            for p in range(lo, lo + n):
                own_in[v, h, p] = ag[v][h][table[h * SIDE, p]]

    def listed_sent(v, g):
        for o in range(1, SIDE):
            for h in range(2):
                listed(v, h, o, g).wait_send()

    def zpart(v, o, lo, n):
        return zed.at[pl.ds((v * SIDE + turn(z, o)) * NP + lo, n)]

    def z_copy(v, o, e, g):
        lo, n = GROUPS[g]
        return remote(zpart(v, o, lo, n), zpart(v, o, lo, n), z_send.at[v, e, g], z_recv.at[v, e, g], z_dev[step[e]])

    def z_direct(v, o, g):
        lo, n = GROUPS[g]
        return remote(zpart(v, o, lo, n), zpart(v, o, lo, n), zf_send.at[v, 0, g], zf_recv.at[v, 0, g], z_dev[2])

    def z_forward(v, o, e, g):
        lo, n = GROUPS[g]
        return remote(
            zpart(v, o, lo + e * (n // 2), n // 2), zpart(v, o, lo + e * (n // 2), n // 2),
            zf_send.at[v, e, g], zf_recv.at[v, e, g], z_dev[step[e]],
        )

    def listed_in(v, g):
        lo, n = GROUPS[g]
        for h in range(2):
            pos = routes[h][0]
            for o in range(1, SIDE):
                listed(v, h, o, g).wait_recv()
            for p in range(lo, lo + n):
                who = table[h * SIDE, NP + p]
                value = own_in[v, h, p]
                for o in range(1, SIDE):
                    value = jnp.where(who == turn(pos, SIDE - o), main_in[v, h, o - 1, p], value)
                zed[(v * SIDE + z) * NP + p, h * half:(h + 1) * half] = value
        for e in range(2):
            go(z_copy(v, 0, e, g))
        if (v, g) in DIRECT:
            go(z_direct(v, 0, g))

    def hand_on(v, g):
        for e in range(2):
            o = (BELOW, ABOVE)[e]
            z_copy(v, o, e, g).wait_recv()
            if (v, g) not in DIRECT:
                go(z_forward(v, o, e, g))

    def arrive(v, g):
        if (v, g) in DIRECT:
            z_direct(v, 2, g).wait_recv()
            return
        for e in range(2):
            z_forward(v, 2, e, g).wait_recv()

    def u_part(o, n):
        return u_all.at[turn(z, o), n]

    def u_copy(o, e, n):
        return remote(u_part(o, n), u_part(o, n), pan_send.at[e, n], pan_recv.at[e, n], z_dev[step[e]])

    def u_forward(o, e):
        return remote(u_part(o, e), u_part(o, e), pan_fsend.at[e], pan_frecv.at[e], z_dev[step[e]])

    def split_u(o):
        for n in range(2):
            at_k = turn(z, o)
            u_high[at_k, :, n * width:(n + 1) * width], u_low[at_k, :, n * width:(n + 1) * width] = parts(u_all[at_k, n])

    def fill(n, carry):
        o = lax.rem(n, SIDE)
        along_x = n // SIDE
        item = at(turn(x, o * along_x), turn(y, o * (1 - along_x)), c)
        for p, (i, k) in enumerate(PAIRS):
            row, dist, swap = locate(structure[i, item], structure[k, item])
            rx, ry, rc = place(row)
            table[n, p] = (jnp.where(along_x == 0, rx, ry) * CORES + rc) * NEAR + dist
            table[n, NP + p] = jnp.where(along_x == 0, ry, rx)
            table[n, 2 * NP + p] = swap.astype(jnp.int32)
        return carry

    def products(p):
        i, k = PAIRS[p]
        block = jnp.concatenate(
            [zed[(v * SIDE + q) * NP + p] for q in range(SIDE) for v in range(PARTS)], axis=0
        )
        flipped = block.T
        swap = table[0, 2 * NP + p] == 1
        direct = parts(jnp.where(swap, flipped, block))
        value = mul(direct, (u_high[k], u_low[k]))
        w[i] = value if i == 0 and k == 0 else w[i] + value
        if i != k:
            value = mul(parts(jnp.where(swap, block, flipped)), (u_high[i], u_low[i]))
            w[k] = value if i == 0 else w[k] + value
        if k == POSITIONS - 1:
            one = (u_high[i, :, :width], u_low[i, :, :width])
            two = (u_high[i, :, width:], u_low[i, :, width:])
            w_one, w_two = parts(w[i, :, :width]), parts(w[i, :, width:])
            diag_one[...] += mul(one, w_one, 0, 0)
            cross = mul(two, w_one, 0, 0)
            mixed[...] = cross if i == 0 else mixed[...] + cross
            rest_two[...] += mul(two, w_two, 0, 0)

    for cp in own_rows[:part // 8]:
        cp.wait()
    for h in range(2):
        reblock(0, h)
        own_out(0, h)
    for cp in loads:
        cp.wait()
    inv_one, inv_two = parts(loaded[1]), parts(loaded[3])
    u_all[z, 0] = mul(parts(loaded[0]), inv_one)
    u_all[z, 1] = mul(parts(loaded[2]), inv_two)
    for order in range(2):
        for e in range(2):
            go(u_copy(0, e, (order, 1 - order)[e]))
    for cp in own_rows[part // 8:]:
        cp.wait()
    for h in range(2):
        reblock(1, h)
    lax.fori_loop(0, 2 * SIDE, fill, 0)
    def both(f):
        def run(v):
            for h in range(2):
                f(v, h)

        return run

    def u_on():
        for e in range(2):
            o = (BELOW, ABOVE)[e]
            u_copy(o, e, e).wait_recv()
            go(u_forward(o, e))

    def u_in():
        for e in range(2):
            u_copy((BELOW, ABOVE)[e], e, 1 - e).wait_recv()
            u_forward(2, e).wait_recv()

    def squares():
        diag_one[...] = mul(inv_one, inv_one, 0, 0)
        rest_two[...] = mul(inv_two, inv_two, 0, 0)

    def u_parent():
        par[...] = mul(parts(loaded[4]), inv_two)

    def multiply(g):
        lo, n = GROUPS[g]
        for p in range(lo, lo + n):
            products(p)

    steps = {
        "O": both(own_out), "F": both(first_in), "S": both(second_in), "R": both(far_in), "T": both(twins_in),
        "L": listed_out, "K": listed_sent, "I": listed_in, "H": hand_on, "A": arrive, "P": multiply,
        "U": u_on, "V": u_in, "D": squares, "Q": u_parent, "X": split_u,
    }
    for name, *at_what in SEQUENCE:
        steps[name](*at_what)
    for v in range(PARTS):
        for g in range(len(GROUPS)):
            if ("K", v, g) not in SEQUENCE:
                listed_sent(v, g)
    own_w[...] = w[z]
    for cp in sent:
        cp.wait_send()


def exchange(structure, root, panel_one, panel_two, inverse_one, parent, inverse_two):
    width = panel_one.shape[0]
    quarter = width // SIDE
    part = quarter // PARTS
    half = part // 2
    f32 = jnp.float32
    dma = pltpu.SemaphoreType.DMA
    hbm = pl.BlockSpec(memory_space=pltpu.HBM)
    vmem = pl.BlockSpec(memory_space=pltpu.VMEM)
    groups = len(GROUPS)
    square = jax.ShapeDtypeStruct((width, width), f32)
    gathered = pltpu.VMEM((SIDE * CORES * NEAR, half, width), f32)
    return pl.pallas_call(
        exchange_kernel,
        out_shape=(jax.ShapeDtypeStruct((width, 2 * width), f32),) + (square,) * 4,
        in_specs=[pl.BlockSpec(memory_space=pltpu.SMEM)] + [hbm] * 6,
        out_specs=(vmem,) * 5,
        scratch_shapes=[
            pltpu.VMEM((PARTS * SIDE * NP, part, width), f32),
            pltpu.VMEM((5, width, width), f32),
            pltpu.VMEM((POSITIONS, 2, width, width), f32),
            pltpu.VMEM((POSITIONS, width, 2 * width), jnp.bfloat16),
            pltpu.VMEM((POSITIONS, width, 2 * width), jnp.bfloat16),
            pltpu.VMEM((POSITIONS, width, 2 * width), f32),
            pltpu.SMEM((2 * SIDE, 3 * NP), jnp.int32),
            pltpu.VMEM((quarter, root.shape[1]), f32),
            gathered, gathered, gathered, gathered,
            pltpu.VMEM((PARTS, 2, SIDE - 1, NP, half, width), f32),
            pltpu.VMEM((PARTS, 2, SIDE - 1, NP, half, width), f32),
            pltpu.VMEM((PARTS, 2, NP, half, width), f32),
            dma((quarter // 8,)),
            dma((5,)),
            dma((2, 2)), dma((2, 2)), dma((2,)), dma((2,)),
            dma((PARTS, 2, 2, 2)), dma((PARTS, 2, 2, 2)), dma((PARTS, 2, 2)), dma((PARTS, 2, 2)),
            dma((PARTS, 2, SIDE, 2)), dma((PARTS, 2, SIDE, 2)),
            dma((PARTS, 2, SIDE - 1, groups)), dma((PARTS, 2, SIDE - 1, groups)),
            dma((PARTS, 2, groups)), dma((PARTS, 2, groups)), dma((PARTS, 2, groups)), dma((PARTS, 2, groups)),
        ],
        compiler_params=pltpu.CompilerParams(
            collective_id=0, has_side_effects=True, vmem_limit_bytes=57 * 2**20
        ),
        name="exchange",
    )(structure, root, panel_one, panel_two, inverse_one, parent, inverse_two)


def finish_kernel(w, total_one, mixed, rest_two, par, diag_one, off_one, diag_two, par_two, root_two):
    width = par.shape[0]
    u_par = parts(par[...])
    w_one = w[:, :width]
    diag_one[...] = total_one[...]
    off_one[...] = -w_one
    root_two[...] = mul(parts(w_one), u_par) - w[:, width:]
    cross = mixed[...]
    p_two = cross.T - mul(parts(total_one[...]), u_par)
    par_two[...] = p_two
    diag_two[...] = rest_two[...] - mul(parts(cross), u_par) - mul(u_par, parts(p_two), 0, 0)


def finish(*args):
    vmem = pl.BlockSpec(memory_space=pltpu.VMEM)
    return pl.pallas_call(
        finish_kernel,
        out_shape=(jax.ShapeDtypeStruct(args[-1].shape, jnp.float32),) * 5,
        in_specs=[vmem] * 5,
        out_specs=(vmem,) * 5,
        compiler_params=pltpu.CompilerParams(vmem_limit_bytes=60 * 2**20),
        name="finish",
    )(*args)


def per_device(root_inverse, structure, panel_one, inverse_one, parent_two, panel_two, inverse_two):
    sums = exchange(
        structure.T, root_inverse, panel_one[0], panel_two[0], inverse_one[0], parent_two[0], inverse_two[0]
    )
    return tuple(out[None] for out in finish(*sums))


def solution(mesh):
    return jax.shard_map(
        per_device,
        mesh=mesh,
        in_specs=(
            P("sn", None),
            P(),
            P("sn", "blk", None),
            P("sn", None, None),
            P("sn", None, None),
            P("sn", "blk", None),
            P("sn", None, None),
        ),
        out_specs=(
            P("sn", None, None),
            P("sn", "blk", None),
            P("sn", None, None),
            P("sn", None, None),
            P("sn", "blk", None),
        ),
        check_vma=False,
    )
```
